32 devices in a mesh: view: 8 (over z, x), slab: 4 (over y, core).
Axes of the slice: x: 2, y: 2, z: 4, core: 2. Of those that a mesh axis runs over, the one named last changes fastest.
Arguments:
- leaf_coeffs: float32 [16, 64, 768], P('view', 'slab'), may hold values from -6 to 6
- measured: float32 [16, 64, 768], P('view', 'slab'), may hold values from -6 to 6
- ray_weight: float32 [16, 64, 768], P('view', 'slab'), may hold values from 0.25 to 1
- cone_weight: float32 [16, 9], P('view'), may hold values from 0.1 to 0.5
- interp_weight: float32 [3, 2, 16, 4], replicated, may hold values from -2 to 2
- shift_offset: int32 [3, 2, 16], replicated, may hold values from -24 to 24
- source_view: int32 [3, 2, 16], replicated, may hold values from 0 to 1
Outputs:
- residual: float32 [16, 64, 768], P('view', 'slab')
- updated: float32 [16, 64, 768], P('view', 'slab')
The draws below stay inside these ranges and needn't reach their ends.
Inputs may be any that keep to these rules, and one draw needn't show every extreme that they name: source_view[l, c, v] is a view row within the supplying block.
All inputs are finite; a program needn't handle non-finite values.
Results may differ from the reference program's by a relative error of at most 0.00012.
Values sent between devices are 32-bit elements; how exact they have to be, the bound alone decides.
No kernel may reach another device: no remote copies, remote signals or barrier semaphores. Data moves between devices by JAX's collectives and lax.ppermute only.
A program may use at most 64 MiB of HBM per device.

```python
import math
import jax
import jax.numpy as jnp
from jax import lax

U = 768
Q = 2
TAPS = 4
REACH = 4
SHIFT = 24
LEVELS = 3
NVIEWS = 16
NZ = 64


def with_ends(entries, rng, smallest, largest):
    longest = entries.shape.index(max(entries.shape))
    spots = []
    for shift in (0, 1):
        where = [jax.random.randint(jax.random.fold_in(rng, axis), (), 0, length) for axis, length in enumerate(entries.shape)]
        where[longest] = (where[longest] + shift) % entries.shape[longest]
        spots.append(tuple(where))
    return entries.at[spots[0]].set(smallest).at[spots[1]].set(largest)


def levels(stream_key, shape, pieces, least, largest):
    def one(axis_at, shards_of):
        heights = jax.random.uniform(jax.random.fold_in(jax.random.fold_in(stream_key, 6), axis_at), (shards_of,), jnp.float32, least / len(pieces), largest / len(pieces))
        return jnp.repeat(jnp.exp(heights), shape[axis_at] // shards_of).reshape((-1,) + (1,) * (len(shape) - axis_at - 1))

    factor_of = one(*pieces[0])
    for cut in pieces[1:]:
        factor_of = factor_of * one(*cut)
    return factor_of


def scatter_about(stream_key, shape, deviation, most, pieces=(), held_as=jnp.bfloat16):
    entries = jax.random.normal(stream_key, shape, jnp.float32) * deviation
    if len(pieces) > 0:
        entries = levels(stream_key, shape, pieces, -0.22, 0.18) * entries
    return jnp.clip(entries, min=-most, max=most).astype(held_as)


def setup_inputs(seed: int = 0) -> dict:
    key_list = jax.random.split(jax.random.key(seed), 8)
    return {
        "leaf_coeffs": scatter_about(key_list[0], (NVIEWS, NZ, U), 1.0, 6.0, ((0, 8), (1, 4)), jnp.float32),
        "measured": scatter_about(key_list[1], (NVIEWS, NZ, U), 1.0, 6.0, ((0, 8), (1, 4)), jnp.float32),
        "ray_weight": jnp.clip(jnp.exp(math.log(1.0) - 1.3862944 * jax.random.uniform(key_list[2], (NVIEWS, NZ, U), jnp.float32) ** levels(key_list[2], (NVIEWS, NZ, U), ((0, 8), (1, 4)), -0.2, 0.2)), 0.25, 1.0),
        "cone_weight": jnp.clip(0.1 + 0.4 * jax.random.uniform(key_list[3], (NVIEWS, 2 * REACH + 1), jnp.float32) ** levels(key_list[3], (NVIEWS, 2 * REACH + 1), ((0, 8),), -0.2, 0.2), 0.1, 0.5),
        "interp_weight": scatter_about(key_list[4], (LEVELS, 2, NVIEWS, TAPS), 0.35, 2.0, (), jnp.float32),
        "shift_offset": with_ends(jax.random.randint(key_list[5], (LEVELS, 2, NVIEWS), 0 - SHIFT, SHIFT + 1), jax.random.fold_in(key_list[5], 1), 0 - SHIFT, SHIFT).astype(jnp.int32),
        "source_view": with_ends(jax.random.randint(key_list[6], (LEVELS, 2, NVIEWS), 0, Q), jax.random.fold_in(key_list[6], 1), 0, Q - 1).astype(jnp.int32),
    }


def slide_rows(whole_block, starts, columns):

    def single_row(row_block, begin_at):
        return lax.dynamic_slice_in_dim(row_block, begin_at, columns, 1)
    return jax.vmap(single_row)(whole_block, starts)

def split_level(current, level_index, interp_weight, shift_offset, source_view):
    stride = 2 ** level_index
    row_ids = jnp.arange(NVIEWS, dtype=jnp.int32)
    owner_device = row_ids // Q
    partner = owner_device + stride - 2 * stride * (owner_device // stride % 2)
    margin = SHIFT + TAPS
    combined = jnp.zeros(current.shape, jnp.float32)
    for channel in range(2):
        supplier = owner_device if channel == 0 else partner
        picked = current[(supplier * Q + source_view[level_index, channel]).astype(jnp.int32)]
        padded = jnp.pad(picked, ((0, 0), (0, 0), (margin, margin)))
        for tap_index in range(TAPS):
            starts = (shift_offset[level_index, channel] + tap_index + margin).astype(jnp.int32)
            shifted = slide_rows(padded, starts, U)
            combined = combined + interp_weight[level_index, channel, :, tap_index][:, None, None] * shifted
    return combined

def tilt_planes(current, cone_weight):
    padded = jnp.pad(current, ((0, 0), (REACH, REACH), (0, 0)))
    combined = jnp.zeros(current.shape, jnp.float32)
    for cone_index in range(2 * REACH + 1):
        combined = combined + cone_weight[:, cone_index][:, None, None] * padded[:, cone_index:cone_index + NZ]
    return combined

def reference(leaf_coeffs, measured, ray_weight, cone_weight, interp_weight, shift_offset, source_view):

    def project(coeffs):
        current = coeffs
        for level_index in range(LEVELS):
            current = split_level(current, level_index, interp_weight, shift_offset, source_view)
        return tilt_planes(current, cone_weight)
    projection, pullback = jax.vjp(project, leaf_coeffs)
    residual = measured - projection
    weighted = ray_weight * residual
    backprojected, = pullback(weighted)
    return (residual, leaf_coeffs + backprojected)
```

```python
import functools

import jax
import jax.numpy as jnp
from jax import lax
from jax.experimental import pallas as pl
from jax.experimental.pallas import tpu as pltpu
from jax.sharding import PartitionSpec as P

LANES = 128
SHIFT = 24


def shifted_sum(rows, moves, weights, total):
    planes, columns = rows.shape
    count = columns // LANES
    tiles = [rows[:, LANES * j : LANES * (j + 1)] for j in range(count)]
    lane = lax.broadcasted_iota(jnp.int32, (planes, LANES), 1)
    nothing = jnp.zeros((planes, LANES), jnp.float32)
    for move, weight in zip(moves, weights):
        turned = [pltpu.roll(tile, (LANES - move) & (LANES - 1), 1) for tile in tiles]
        below = lane + move < 0
        above = lane + move >= LANES
        for j in range(count):
            left = turned[j - 1] if j > 0 else nothing
            right = turned[j + 1] if j + 1 < count else nothing
            term = weight * jnp.where(below, left, jnp.where(above, right, turned[j]))
            total[j] = term if total[j] is None else total[j] + term
    return total


def join(tiles):
    return jnp.concatenate(tiles, axis=1)


def level_forward(level, block, own, partner, out, params):
    weight, offset, source = params
    views, _, columns = own.shape
    taps = weight.shape[3]
    for v in range(views):
        row = block * views + v
        total = [None] * (columns // LANES)
        for channel, held in enumerate((own, partner)):
            begin = offset[level, channel, row]
            total = shifted_sum(
                held[source[level, channel, row]],
                [begin + k for k in range(taps)],
                [weight[level, channel, row, k] for k in range(taps)],
                total,
            )
        out[v] = join(total)


def level_back(level, block, own, partner, out, params):
    weight, offset, source = params
    views, _, columns = own.shape
    taps = weight.shape[3]
    out[...] = jnp.zeros(out.shape, jnp.float32)
    for channel, held in enumerate((own, partner)):
        owner = block ^ (channel << level)
        for v in range(views):
            row = owner * views + v
            begin = offset[level, channel, row]
            total = shifted_sum(
                held[v],
                [-begin - k for k in range(taps)],
                [weight[level, channel, row, k] for k in range(taps)],
                [None] * (columns // LANES),
            )
            target = source[level, channel, row]
            out[target] = out[target] + join(total)


def forward_kernel(levels, count, last, weight, offset, source, *refs):
    params = (weight, offset, source)
    states, refs = refs[:count], refs[count:]
    out = refs[0]
    me = lax.axis_index("view")
    if len(levels) == 2:
        near, far = refs[-2:]
        low, high = levels
        level_forward(low, me, states[0], states[1], near, params)
        level_forward(low, me ^ (1 << high), states[2], states[3], far, params)
        level_forward(high, me, near, far, out, params)
    else:
        level_forward(levels[0], me, states[0], states[1], out, params)
    if last:
        pair, across = refs[1:3]
        width = pair.shape[1]
        planes = out.shape[1]
        odd = lax.axis_index("slab") % 2
        top = pl.multiple_of((1 - odd) * (planes - width), 8)
        bottom = pl.multiple_of(odd * (planes - width), 8)
        pair[...] = out[:, pl.ds(top, width), :]
        across[...] = out[:, pl.ds(bottom, width), :]


def back_kernel(levels, count, last, weight, offset, source, *refs):
    params = (weight, offset, source)
    states, refs = refs[:count], refs[count:]
    me = lax.axis_index("view")
    if last:
        leaf, refs = refs[0], refs[1:]
    out = refs[0]
    if len(levels) == 2:
        near, far = refs[-2:]
        low, high = levels
        level_back(high, me, states[0], states[2], near, params)
        level_back(high, me ^ (1 << low), states[1], states[3], far, params)
        level_back(low, me, near, far, out, params)
    else:
        level_back(levels[0], me, states[0], states[1], out, params)
    if last:
        out[...] = leaf[...] + out[...]


def tilt_kernel(cone, split, pair, across, measured, ray, residual, cotangent, wide, weighted):
    views, planes, columns = split.shape
    width = pair.shape[1]
    crossed = cone.shape[1]
    reach = crossed // 2
    odd = lax.axis_index("slab") % 2
    far = planes + width
    wide[:, pl.ds(width, planes), :] = split[...]
    wide[:, pl.ds(pl.multiple_of((1 - odd) * far, 8), width), :] = pair[...]
    wide[:, pl.ds(pl.multiple_of(odd * far, 8), width), :] = across[...]
    extended = planes + 2 * reach
    for v in range(views):
        for j in range(columns // LANES):
            at = pl.ds(LANES * j, LANES)
            total = cone[v, 0] * wide[v, pl.ds(width - 2 * reach, extended), at]
            for e in range(1, crossed):
                total = total + cone[v, e] * wide[v, pl.ds(width - 2 * reach + e, extended), at]
            left = measured[v, :, at] - total
            residual[v, :, at] = left[reach : reach + planes]
            weighted[v, :, at] = ray[v, :, at] * left
            total = cone[v, 0] * weighted[v, pl.ds(2 * reach, planes), at]
            for e in range(1, crossed):
                total = total + cone[v, e] * weighted[v, pl.ds(2 * reach - e, planes), at]
            cotangent[v, :, at] = total


SCALARS = pl.BlockSpec(memory_space=pltpu.SMEM)
BLOCK = pl.BlockSpec(memory_space=pltpu.VMEM)


def shaped(*shape):
    return jax.ShapeDtypeStruct(shape, jnp.float32)


def across_view(x, apart):
    return lax.ppermute(x, "view", [(i, i ^ apart) for i in range(lax.axis_size("view"))])


def with_pair(x):
    return lax.ppermute(x, "slab", [(i, i ^ 1) for i in range(lax.axis_size("slab"))])


def across_pairs(x):
    lower = range(1, lax.axis_size("slab") - 1, 2)
    return lax.ppermute(x, "slab", [(i, i + 1) for i in lower] + [(i + 1, i) for i in lower])


def gathered(x, levels):
    steps = [1 << level for level in levels]
    if len(steps) == 2:
        steps.append(steps[0] + steps[1])
    return [x] + [across_view(x, step) for step in steps]


def body(leaf_coeffs, measured, ray_weight, cone_weight, interp_weight, shift_offset, source_view):
    views, planes, columns = leaf_coeffs.shape
    reach = cone_weight.shape[1] // 2
    level_count = lax.axis_size("view").bit_length() - 1
    groups = [tuple(range(i, min(i + 2, level_count))) for i in range(0, level_count, 2)]
    params = (interp_weight, shift_offset, source_view)
    whole = shaped(views, planes, columns)
    part = shaped(views, 2 * reach, columns)
    scratch = [pltpu.VMEM((views, planes, columns), jnp.float32)] * 2

    odd = lax.axis_index("slab") % 2 == 1
    both = jnp.stack([measured, ray_weight])
    low, high = both[:, :, :reach], both[:, :, planes - reach :]
    paired = with_pair(jnp.where(odd, low, high))
    crossing = across_pairs(jnp.where(odd, high, low))
    both = jnp.concatenate(
        [jnp.where(odd, paired, crossing), both, jnp.where(odd, crossing, paired)], axis=2
    )

    state = leaf_coeffs
    for levels in groups:
        states = gathered(state, levels)
        last = levels == groups[-1]
        state = pl.pallas_call(
            functools.partial(forward_kernel, levels, len(states), last),
            out_shape=[whole] + [part] * 2 * last,
            in_specs=[SCALARS] * 3 + [BLOCK] * len(states),
            out_specs=[BLOCK] * (1 + 2 * last),
            scratch_shapes=scratch if len(levels) == 2 else [],
            name="split",
        )(*params, *states)
        if last:
            split, to_pair, to_across = state
        else:
            state = state[0]

    residual, cotangent = pl.pallas_call(
        tilt_kernel,
        out_shape=[whole, whole],
        in_specs=[SCALARS] + [BLOCK] * 5,
        out_specs=[BLOCK] * 2,
        scratch_shapes=[
            pltpu.VMEM((views, planes + 4 * reach, columns), jnp.float32),
            pltpu.VMEM((views, planes + 2 * reach, columns), jnp.float32),
        ],
        name="tilt",
    )(cone_weight, split, with_pair(to_pair), across_pairs(to_across), both[0], both[1])

    state = cotangent
    for levels in reversed(groups):
        states = gathered(state, levels)
        last = levels == groups[0]
        state = pl.pallas_call(
            functools.partial(back_kernel, levels, len(states), last),
            out_shape=whole,
            in_specs=[SCALARS] * 3 + [BLOCK] * (len(states) + last),
            out_specs=BLOCK,
            scratch_shapes=scratch if len(levels) == 2 else [],
            name="back",
        )(*params, *states, *([leaf_coeffs] if last else []))
    return (residual, state)


def solution(mesh):
    in_specs = (
        P("view", "slab", None),
        P("view", "slab", None),
        P("view", "slab", None),
        P("view", None),
        P(),
        P(),
        P(),
    )
    out_specs = (P("view", "slab", None), P("view", "slab", None))
    return jax.shard_map(body, mesh=mesh, in_specs=in_specs, out_specs=out_specs, check_vma=False)
```

```python
import functools

import jax
import jax.numpy as jnp
from jax import lax
from jax.experimental import pallas as pl
from jax.experimental.pallas import tpu as pltpu
from jax.sharding import PartitionSpec as P

LANES = 128
SHIFT = 24


def shifted_sum(rows, moves, weights, total):
    planes, columns = rows.shape
    count = columns // LANES
    tiles = [rows[:, LANES * j : LANES * (j + 1)] for j in range(count)]
    lane = lax.broadcasted_iota(jnp.int32, (planes, LANES), 1)
    nothing = jnp.zeros((planes, LANES), jnp.float32)
    for move, weight in zip(moves, weights):
        turned = [pltpu.roll(tile, (LANES - move) & (LANES - 1), 1) for tile in tiles]
        below = lane + move < 0
        above = lane + move >= LANES
        for j in range(count):
            left = turned[j - 1] if j > 0 else nothing
            right = turned[j + 1] if j + 1 < count else nothing
            term = weight * jnp.where(below, left, jnp.where(above, right, turned[j]))
            total[j] = term if total[j] is None else total[j] + term
    return total


def join(tiles):
    return jnp.concatenate(tiles, axis=1)


def level_forward(level, block, own, partner, out, params):
    weight, offset, source = params
    views, _, columns = own.shape
    taps = weight.shape[2]
    for v in range(views):
        row = block * views + v
        total = [None] * (columns // LANES)
        for channel, held in enumerate((own, partner)):
            begin = offset[level, channel, row]
            total = shifted_sum(
                held[source[level, channel, row]],
                [begin + k for k in range(taps)],
                [weight[level, channel, k, row] for k in range(taps)],
                total,
            )
        out[v] = join(total)


def level_back(level, block, own, partner, out, params):
    weight, offset, source = params
    views, _, columns = own.shape
    taps = weight.shape[2]
    out[...] = jnp.zeros(out.shape, jnp.float32)
    for channel, held in enumerate((own, partner)):
        owner = block ^ (channel << level)
        for v in range(views):
            row = owner * views + v
            begin = offset[level, channel, row]
            total = shifted_sum(
                held[v],
                [-begin - k for k in range(taps)],
                [weight[level, channel, k, row] for k in range(taps)],
                [None] * (columns // LANES),
            )
            target = source[level, channel, row]
            out[target] = out[target] + join(total)


def forward_kernel(levels, count, last, weight, offset, source, *refs):
    params = (weight, offset, source)
    states, refs = refs[:count], refs[count:]
    out = refs[0]
    me = lax.axis_index("view")
    if len(levels) == 2:
        near, far = refs[-2:]
        low, high = levels
        level_forward(low, me, states[0], states[1], near, params)
        level_forward(low, me ^ (1 << high), states[2], states[3], far, params)
        level_forward(high, me, near, far, out, params)
    else:
        level_forward(levels[0], me, states[0], states[1], out, params)
    if last:
        pair, across = refs[1:3]
        width = pair.shape[1]
        planes = out.shape[1]
        odd = lax.axis_index("slab") % 2
        top = pl.multiple_of((1 - odd) * (planes - width), 8)
        bottom = pl.multiple_of(odd * (planes - width), 8)
        pair[...] = out[:, pl.ds(top, width), :]
        across[...] = out[:, pl.ds(bottom, width), :]


def back_kernel(levels, count, last, weight, offset, source, *refs):
    params = (weight, offset, source)
    states, refs = refs[:count], refs[count:]
    me = lax.axis_index("view")
    if last:
        leaf, refs = refs[0], refs[1:]
    out = refs[0]
    if len(levels) == 2:
        near, far = refs[-2:]
        low, high = levels
        level_back(high, me, states[0], states[2], near, params)
        level_back(high, me ^ (1 << low), states[1], states[3], far, params)
        level_back(low, me, near, far, out, params)
    else:
        level_back(levels[0], me, states[0], states[1], out, params)
    if last:
        out[...] = leaf[...] + out[...]


def tilt_kernel(cone, split, pair, across, measured, ray, residual, cotangent, wide, weighted):
    views, planes, columns = split.shape
    width = pair.shape[1]
    crossed = cone.shape[1]
    reach = crossed // 2
    odd = lax.axis_index("slab") % 2
    far = planes + width
    wide[:, pl.ds(width, planes), :] = split[...]
    wide[:, pl.ds(pl.multiple_of((1 - odd) * far, 8), width), :] = pair[...]
    wide[:, pl.ds(pl.multiple_of(odd * far, 8), width), :] = across[...]
    extended = planes + 2 * reach
    for v in range(views):
        for j in range(columns // LANES):
            at = pl.ds(LANES * j, LANES)
            total = cone[v, 0] * wide[v, pl.ds(width - 2 * reach, extended), at]
            for e in range(1, crossed):
                total = total + cone[v, e] * wide[v, pl.ds(width - 2 * reach + e, extended), at]
            left = measured[v, :, at] - total
            residual[v, :, at] = left[reach : reach + planes]
            weighted[v, :, at] = ray[v, :, at] * left
            total = cone[v, 0] * weighted[v, pl.ds(2 * reach, planes), at]
            for e in range(1, crossed):
                total = total + cone[v, e] * weighted[v, pl.ds(2 * reach - e, planes), at]
            cotangent[v, :, at] = total


SCALARS = pl.BlockSpec(memory_space=pltpu.SMEM)
BLOCK = pl.BlockSpec(memory_space=pltpu.VMEM)
SMALL = pltpu.CompilerParams(vmem_limit_bytes=8 << 20)


def shaped(*shape):
    return jax.ShapeDtypeStruct(shape, jnp.float32)


def across_view(x, apart):
    return lax.ppermute(x, "view", [(i, i ^ apart) for i in range(lax.axis_size("view"))])


def with_pair(x):
    return lax.ppermute(x, "slab", [(i, i ^ 1) for i in range(lax.axis_size("slab"))])


def across_pairs(x):
    lower = range(1, lax.axis_size("slab") - 1, 2)
    return lax.ppermute(x, "slab", [(i, i + 1) for i in lower] + [(i + 1, i) for i in lower])


def gathered(x, levels):
    steps = [1 << level for level in levels]
    if len(steps) == 2:
        steps.append(steps[0] + steps[1])
    return [x] + [across_view(x, step) for step in steps]


def body(leaf_coeffs, measured, ray_weight, cone_weight, interp_weight, shift_offset, source_view):
    views, planes, columns = leaf_coeffs.shape
    reach = cone_weight.shape[1] // 2
    level_count = lax.axis_size("view").bit_length() - 1
    groups = [tuple(range(i, min(i + 2, level_count))) for i in range(0, level_count, 2)]
    params = (jnp.swapaxes(interp_weight, 2, 3), shift_offset, source_view)
    whole = shaped(views, planes, columns)
    part = shaped(views, 2 * reach, columns)
    scratch = [pltpu.VMEM((views, planes, columns), jnp.float32)] * 2

    odd = lax.axis_index("slab") % 2 == 1
    both = jnp.stack([measured, ray_weight])
    low, high = both[:, :, :reach], both[:, :, planes - reach :]
    paired = with_pair(jnp.where(odd, low, high))
    crossing = across_pairs(jnp.where(odd, high, low))
    both = jnp.concatenate(
        [jnp.where(odd, paired, crossing), both, jnp.where(odd, crossing, paired)], axis=2
    )

    state = leaf_coeffs
    for levels in groups:
        states = gathered(state, levels)
        last = levels == groups[-1]
        state = pl.pallas_call(
            functools.partial(forward_kernel, levels, len(states), last),
            out_shape=[whole] + [part] * 2 * last,
            in_specs=[SCALARS] * 3 + [BLOCK] * len(states),
            out_specs=[BLOCK] * (1 + 2 * last),
            scratch_shapes=scratch if len(levels) == 2 else [],
            compiler_params=SMALL,
            name="split",
        )(*params, *states)
        if last:
            split, to_pair, to_across = state
        else:
            state = state[0]

    residual, cotangent = pl.pallas_call(
        tilt_kernel,
        out_shape=[whole, whole],
        in_specs=[SCALARS] + [BLOCK] * 5,
        out_specs=[BLOCK] * 2,
        scratch_shapes=[
            pltpu.VMEM((views, planes + 4 * reach, columns), jnp.float32),
            pltpu.VMEM((views, planes + 2 * reach, columns), jnp.float32),
        ],
        compiler_params=SMALL,
        name="tilt",
    )(cone_weight, split, with_pair(to_pair), across_pairs(to_across), both[0], both[1])

    state = cotangent
    for levels in reversed(groups):
        states = gathered(state, levels)
        last = levels == groups[0]
        state = pl.pallas_call(
            functools.partial(back_kernel, levels, len(states), last),
            out_shape=whole,
            in_specs=[SCALARS] * 3 + [BLOCK] * (len(states) + last),
            out_specs=BLOCK,
            scratch_shapes=scratch if len(levels) == 2 else [],
            compiler_params=SMALL,
            name="back",
        )(*params, *states, *([leaf_coeffs] if last else []))
    return (residual, state)


def solution(mesh):
    in_specs = (
        P("view", "slab", None),
        P("view", "slab", None),
        P("view", "slab", None),
        P("view", None),
        P(),
        P(),
        P(),
    )
    out_specs = (P("view", "slab", None), P("view", "slab", None))
    return jax.shard_map(body, mesh=mesh, in_specs=in_specs, out_specs=out_specs, check_vma=False)
```

```python
import functools

import jax
import jax.numpy as jnp
from jax import lax
from jax.experimental import pallas as pl
from jax.experimental.pallas import tpu as pltpu
from jax.sharding import PartitionSpec as P

LANES = 128
SCALARS = pl.BlockSpec(memory_space=pltpu.SMEM)
BLOCK = pl.BlockSpec(memory_space=pltpu.VMEM)
SMALL = pltpu.CompilerParams(vmem_limit_bytes=8 << 20)


def shifted_sum(rows, moves, weights, total):
    planes, columns = rows.shape
    count = columns // LANES
    tiles = [rows[:, LANES * j : LANES * (j + 1)] for j in range(count)]
    lane = lax.broadcasted_iota(jnp.int32, (planes, LANES), 1)
    nothing = jnp.zeros((planes, LANES), jnp.float32)
    for move, weight in zip(moves, weights):
        turned = [pltpu.roll(tile, (LANES - move) & (LANES - 1), 1) for tile in tiles]
        below = lane + move < 0
        above = lane + move >= LANES
        for j in range(count):
            left = turned[j - 1] if j > 0 else nothing
            right = turned[j + 1] if j + 1 < count else nothing
            term = weight * jnp.where(below, left, jnp.where(above, right, turned[j]))
            total[j] = term if total[j] is None else total[j] + term
    return total


def table_kernel(entries, views, weight, offset, source, whole_numbers, weights):
    me = lax.axis_index("view")
    taps = weight.shape[2]
    for index, (level, channel, apart, direction) in enumerate(entries):
        for v in range(views):
            row = (me ^ apart) * views + v
            at = index * views + v
            begin = offset[level, channel, row] * direction
            whole_numbers[2 * at, :] = jnp.full((LANES,), begin, jnp.int32)
            whole_numbers[2 * at + 1, :] = jnp.full((LANES,), source[level, channel, row], jnp.int32)
            for k in range(taps):
                weights[at * taps + k, :] = jnp.full((LANES,), weight[level, channel, k, row])


def level_part(index, direction, whole_numbers, weights, given, base, out):
    views, planes, columns = given.shape
    taps = weights.shape[0] // (whole_numbers.shape[0] // 2)
    count = columns // LANES
    if direction < 0:
        out[...] = jnp.zeros(out.shape, jnp.float32) if base is None else base[...]
    for v in range(views):
        at = index * views + v
        begin, source = whole_numbers[2 * at, 0], whole_numbers[2 * at + 1, 0]
        moves = [begin + direction * k for k in range(taps)]
        factors = [
            jnp.broadcast_to(weights[pl.ds(at * taps + k, 1), :], (planes, LANES))
            for k in range(taps)
        ]
        if direction > 0:
            total = [None] * count
            if base is not None:
                total = [base[v, :, LANES * j : LANES * (j + 1)] for j in range(count)]
            total = shifted_sum(given[source], moves, factors, total)
            for j in range(count):
                out[v, :, LANES * j : LANES * (j + 1)] = total[j]
        else:
            total = shifted_sum(given[v], moves, factors, [None] * count)
            out[source] = out[source] + jnp.concatenate(total, axis=1)


def part_kernel(index, direction, based, whole_numbers, weights, given, *refs):
    level_part(index, direction, whole_numbers, weights, given, refs[0] if based else None, refs[-1])


def two_kernel(first, second, direction, whole_numbers, weights, given, base, other, out, between):
    level_part(first, direction, whole_numbers, weights, given, base, between)
    level_part(second, direction, whole_numbers, weights, between, other, out)


def edges_kernel(index, whole_numbers, weights, given, base, out, pair, across):
    level_part(index, 1, whole_numbers, weights, given, base, out)
    width = pair.shape[1]
    planes = out.shape[1]
    odd = lax.axis_index("slab") % 2
    pair[...] = out[:, pl.ds(pl.multiple_of((1 - odd) * (planes - width), 8), width), :]
    across[...] = out[:, pl.ds(pl.multiple_of(odd * (planes - width), 8), width), :]


def tilt_kernel(cone, split, pair, across, measured, ray, residual, cotangent, wide, weighted):
    views, planes, columns = split.shape
    width = pair.shape[1]
    crossed = cone.shape[0] // views
    reach = crossed // 2
    odd = lax.axis_index("slab") % 2
    far = planes + width
    wide[:, pl.ds(width, planes), :] = split[...]
    wide[:, pl.ds(pl.multiple_of((1 - odd) * far, 8), width), :] = pair[...]
    wide[:, pl.ds(pl.multiple_of(odd * far, 8), width), :] = across[...]
    extended = planes + 2 * reach
    for v in range(views):
        factors = [cone[pl.ds(v * crossed + e, 1), :] for e in range(crossed)]
        for j in range(columns // LANES):
            at = pl.ds(LANES * j, LANES)
            total = factors[0] * wide[v, pl.ds(width - 2 * reach, extended), at]
            for e in range(1, crossed):
                total = total + factors[e] * wide[v, pl.ds(width - 2 * reach + e, extended), at]
            left = measured[v, :, at] - total
            residual[v, :, at] = left[reach : reach + planes]
            weighted[v, :, at] = ray[v, :, at] * left
            total = factors[0] * weighted[v, pl.ds(2 * reach, planes), at]
            for e in range(1, crossed):
                total = total + factors[e] * weighted[v, pl.ds(2 * reach - e, planes), at]
            cotangent[v, :, at] = total


def shaped(*shape, dtype=jnp.float32):
    return jax.ShapeDtypeStruct(shape, dtype)


def call(kernel, out_shape, *args, scratch=(), specs=None, name):
    return pl.pallas_call(
        kernel,
        out_shape=out_shape,
        in_specs=[BLOCK] * len(args) if specs is None else specs,
        out_specs=jax.tree.map(lambda _: BLOCK, out_shape),
        scratch_shapes=scratch,
        compiler_params=SMALL,
        name=name,
    )(*args)


def across_view(x, apart):
    return lax.ppermute(x, "view", [(i, i ^ apart) for i in range(lax.axis_size("view"))])


def with_pair(x):
    return lax.ppermute(x, "slab", [(i, i ^ 1) for i in range(lax.axis_size("slab"))])


def across_pairs(x):
    lower = range(1, lax.axis_size("slab") - 1, 2)
    return lax.ppermute(x, "slab", [(i, i + 1) for i in lower] + [(i + 1, i) for i in lower])


def after(x, *earlier):
    return lax.optimization_barrier((x, *earlier))[0]


def body(leaf_coeffs, measured, ray_weight, cone_weight, interp_weight, shift_offset, source_view):
    views, planes, columns = leaf_coeffs.shape
    crossed = cone_weight.shape[1]
    reach = crossed // 2
    taps = interp_weight.shape[3]
    level_count = lax.axis_size("view").bit_length() - 1
    groups = [tuple(range(i, min(i + 2, level_count))) for i in range(0, level_count, 2)]
    whole = shaped(views, planes, columns)
    part = shaped(views, 2 * reach, columns)
    scratch = [pltpu.VMEM((views, planes, columns), jnp.float32)]

    entries = []

    def entry(level, channel, apart, direction):
        entries.append((level, channel, apart, direction))
        return len(entries) - 1

    forward_entries, back_entries = {}, {}
    for levels in groups:
        low, high = levels[0], levels[-1]
        shapes = [(low, 0), (low, 1)]
        if len(levels) == 2:
            shapes = [(low, 0), (low, 1 << high), (high, 0)]
            backs = [(high, 0), (high, 1 << low), (low, 0)]
        else:
            shapes = backs = [(low, 0)]
        forward_entries[levels] = [
            [entry(level, channel, apart, 1) for channel in (0, 1)] for level, apart in shapes
        ]
        back_entries[levels] = [
            [entry(level, channel, apart ^ (channel << level), -1) for channel in (0, 1)]
            for level, apart in backs
        ]
    tables = call(
        functools.partial(table_kernel, entries, views),
        [
            shaped(len(entries) * views * 2, LANES, dtype=jnp.int32),
            shaped(len(entries) * views * taps, LANES),
        ],
        jnp.swapaxes(interp_weight, 2, 3),
        shift_offset,
        source_view,
        specs=[SCALARS] * 3,
        name="tables",
    )
    cone = jnp.broadcast_to(cone_weight.reshape(-1, 1), (views * crossed, LANES))

    def one(index, direction, given, base=None):
        return call(
            functools.partial(part_kernel, index, direction, base is not None),
            whole,
            *tables,
            given,
            *(() if base is None else (base,)),
            name="part",
        )

    def two(first, second, direction, given, base, other):
        return call(
            functools.partial(two_kernel, first, second, direction),
            whole,
            *tables,
            given,
            base,
            other,
            scratch=scratch,
            name="two_parts",
        )

    def pair_group(steps, direction, state, first, second, third, base=None):
        near, far, joined = steps
        near_sum = one(near[0], direction, state)
        near_sum = one(near[1], direction, first, near_sum)
        far_sum = one(far[0], direction, second)
        joined_sum = one(joined[0], direction, near_sum, base)
        return two(far[1], joined[1], direction, third, far_sum, joined_sum)

    state = leaf_coeffs
    for levels in groups:
        steps = forward_entries[levels]
        near = 1 << levels[0]
        if len(levels) == 2:
            far = 1 << levels[1]
            received = [across_view(state, apart) for apart in (near, far, near + far)]
            state = pair_group(steps, 1, state, *received)
            begun = state
        else:
            received = across_view(state, near)
            begun = one(steps[0][0], 1, state)
            if levels != groups[-1]:
                state = one(steps[0][1], 1, received, begun)
            else:
                state, to_pair, to_across = call(
                    functools.partial(edges_kernel, steps[0][1]),
                    [whole, part, part],
                    *tables,
                    received,
                    begun,
                    name="edges",
                )

    odd = lax.axis_index("slab") % 2 == 1
    both = jnp.stack([measured, ray_weight])
    both = after(both, begun)
    low, high = both[:, :, :reach], both[:, :, planes - reach :]
    paired = with_pair(jnp.where(odd, low, high))
    crossing = across_pairs(jnp.where(odd, high, low))
    both = jnp.concatenate(
        [jnp.where(odd, paired, crossing), both, jnp.where(odd, crossing, paired)], axis=2
    )

    from_across = across_pairs(to_across)
    from_pair = with_pair(to_pair)
    residual, cotangent = call(
        tilt_kernel,
        [whole, whole],
        cone,
        state,
        from_pair,
        from_across,
        both[0],
        both[1],
        scratch=[
            pltpu.VMEM((views, planes + 4 * reach, columns), jnp.float32),
            pltpu.VMEM((views, planes + 2 * reach, columns), jnp.float32),
        ],
        name="tilt",
    )

    state = cotangent
    for levels in reversed(groups):
        steps = back_entries[levels]
        near = 1 << levels[0]
        base = leaf_coeffs if levels == groups[0] else None
        if len(levels) == 2:
            far = 1 << levels[1]
            received = [across_view(state, apart) for apart in (far, near, near + far)]
            state = pair_group(steps, -1, state, *received, base)
        else:
            received = across_view(state, near)
            begun = one(steps[0][0], -1, state, base)
            state = one(steps[0][1], -1, received, begun)
    return (residual, state)


def solution(mesh):
    in_specs = (
        P("view", "slab", None),
        P("view", "slab", None),
        P("view", "slab", None),
        P("view", None),
        P(),
        P(),
        P(),
    )
    out_specs = (P("view", "slab", None), P("view", "slab", None))
    return jax.shard_map(body, mesh=mesh, in_specs=in_specs, out_specs=out_specs, check_vma=False)
```

```python
import functools

import jax
import jax.numpy as jnp
from jax import lax
from jax.experimental import pallas as pl
from jax.experimental.pallas import tpu as pltpu
from jax.sharding import PartitionSpec as P

LANES = 128
SCALARS = pl.BlockSpec(memory_space=pltpu.SMEM)
BLOCK = pl.BlockSpec(memory_space=pltpu.VMEM)
SMALL = pltpu.CompilerParams(vmem_limit_bytes=8 << 20)


def shifted_sum(rows, moves, weights, total):
    planes, columns = rows.shape
    count = columns // LANES
    tiles = [rows[:, LANES * j : LANES * (j + 1)] for j in range(count)]
    lane = lax.broadcasted_iota(jnp.int32, (planes, LANES), 1)
    nothing = jnp.zeros((planes, LANES), jnp.float32)
    for move, weight in zip(moves, weights):
        turned = [pltpu.roll(tile, (LANES - move) & (LANES - 1), 1) for tile in tiles]
        below = lane + move < 0
        above = lane + move >= LANES
        for j in range(count):
            left = turned[j - 1] if j > 0 else nothing
            right = turned[j + 1] if j + 1 < count else nothing
            term = weight * jnp.where(below, left, jnp.where(above, right, turned[j]))
            total[j] = term if total[j] is None else total[j] + term
    return total


def table_kernel(entries, views, weight, offset, source, cone, whole_numbers, weights, crossing):
    me = lax.axis_index("view")
    taps = weight.shape[2]
    for index, (level, channel, apart, direction) in enumerate(entries):
        for v in range(views):
            row = (me ^ apart) * views + v
            at = index * views + v
            begin = offset[level, channel, row] * direction
            whole_numbers[2 * at, :] = jnp.full((LANES,), begin, jnp.int32)
            whole_numbers[2 * at + 1, :] = jnp.full((LANES,), source[level, channel, row], jnp.int32)
            for k in range(taps):
                weights[at * taps + k, :] = jnp.full((LANES,), weight[level, channel, k, row])
    crossed = cone.shape[1]
    for v in range(views):
        for e in range(crossed):
            crossing[v * crossed + e, :] = jnp.full((LANES,), cone[v, e])


def level_part(index, direction, whole_numbers, weights, given, base, out):
    views, planes, columns = given.shape
    taps = weights.shape[0] // (whole_numbers.shape[0] // 2)
    count = columns // LANES
    if direction < 0:
        out[...] = jnp.zeros(out.shape, jnp.float32) if base is None else base[...]
    for v in range(views):
        at = index * views + v
        begin, source = whole_numbers[2 * at, 0], whole_numbers[2 * at + 1, 0]
        moves = [begin + direction * k for k in range(taps)]
        factors = [
            jnp.broadcast_to(weights[pl.ds(at * taps + k, 1), :], (planes, LANES))
            for k in range(taps)
        ]
        if direction > 0:
            total = [None] * count
            if base is not None:
                total = [base[v, :, LANES * j : LANES * (j + 1)] for j in range(count)]
            total = shifted_sum(given[source], moves, factors, total)
            for j in range(count):
                out[v, :, LANES * j : LANES * (j + 1)] = total[j]
        else:
            total = shifted_sum(given[v], moves, factors, [None] * count)
            out[source] = out[source] + jnp.concatenate(total, axis=1)


def part_kernel(index, direction, based, whole_numbers, weights, given, *refs):
    level_part(index, direction, whole_numbers, weights, given, refs[0] if based else None, refs[-1])


def two_kernel(first, second, direction, whole_numbers, weights, given, base, other, out, between):
    level_part(first, direction, whole_numbers, weights, given, base, between)
    level_part(second, direction, whole_numbers, weights, between, other, out)


def edges_kernel(
    reach, index, whole_numbers, weights, given, base, measured, ray, out, pair, across
):
    level_part(index, 1, whole_numbers, weights, given, base, out)
    views, planes, columns = out.shape
    width = 2 * reach
    odd = lax.axis_index("slab") % 2
    row = lax.broadcasted_iota(jnp.int32, (views, width, columns), 1)
    for message, top in ((pair, 1 - odd), (across, odd)):
        edge = pl.ds(pl.multiple_of(top * (planes - width), width), width)
        message[:, :width] = out[:, edge, :]
        own = (row >= reach) == (top == 1)
        message[:, width:] = jnp.where(own, measured[:, edge], pltpu.roll(ray[:, edge], reach, 1))


def tilt_kernel(
    cone, split, pair, across, measured, ray, residual, cotangent, wide, seen, lengths, weighted
):
    views, planes, columns = split.shape
    width = pair.shape[1] // 2
    reach = width // 2
    crossed = cone.shape[0] // views
    odd = lax.axis_index("slab") % 2
    far = planes + width
    extended = planes + 2 * reach
    own = pl.ds(width, planes)
    for v in range(views):
        factors = [cone[pl.ds(v * crossed + e, 1), :] for e in range(crossed)]
        for j in range(columns // LANES):
            at = pl.ds(LANES * j, LANES)
            wide[v, j, own] = split[v, :, at]
            seen[v, j, own] = measured[v, :, at]
            lengths[v, j, own] = ray[v, :, at]
            for message, side in ((pair, 1 - odd), (across, odd)):
                edge = pl.ds(pl.multiple_of(side * far, width), width)
                mixed = message[v, width:, at]
                wide[v, j, edge] = message[v, :width, at]
                seen[v, j, edge] = mixed
                lengths[v, j, edge] = pltpu.roll(mixed, reach, 0)
            total = factors[0] * wide[v, j, pl.ds(0, extended)]
            for e in range(1, crossed):
                total = total + factors[e] * wide[v, j, pl.ds(e, extended)]
            left = seen[v, j, pl.ds(reach, extended)] - total
            weighted[v, j] = lengths[v, j, pl.ds(reach, extended)] * left
            residual[v, :, at] = left[reach : reach + planes]
            total = factors[0] * weighted[v, j, pl.ds(2 * reach, planes)]
            for e in range(1, crossed):
                total = total + factors[e] * weighted[v, j, pl.ds(2 * reach - e, planes)]
            cotangent[v, :, at] = total


def copy_kernel(given, out):
    out[...] = given[...]


def shaped(*shape, dtype=jnp.float32):
    return jax.ShapeDtypeStruct(shape, dtype)


def call(kernel, out_shape, *args, scratch=(), specs=None, name):
    return pl.pallas_call(
        kernel,
        out_shape=out_shape,
        in_specs=[BLOCK] * len(args) if specs is None else specs,
        out_specs=jax.tree.map(lambda _: BLOCK, out_shape),
        scratch_shapes=scratch,
        compiler_params=SMALL,
        name=name,
    )(*args)


def across_view(x, apart):
    return lax.ppermute(x, "view", [(i, i ^ apart) for i in range(lax.axis_size("view"))])


def with_pair(x):
    return lax.ppermute(x, "slab", [(i, i ^ 1) for i in range(lax.axis_size("slab"))])


def across_pairs(x):
    lower = range(1, lax.axis_size("slab") - 1, 2)
    return lax.ppermute(x, "slab", [(i, i + 1) for i in lower] + [(i + 1, i) for i in lower])


def body(leaf_coeffs, measured, ray_weight, cone_weight, interp_weight, shift_offset, source_view):
    views, planes, columns = leaf_coeffs.shape
    crossed = cone_weight.shape[1]
    reach = crossed // 2
    taps = interp_weight.shape[3]
    level_count = lax.axis_size("view").bit_length() - 1
    groups = [tuple(range(i, min(i + 2, level_count))) for i in range(0, level_count, 2)]
    whole = shaped(views, planes, columns)
    message = shaped(views, 4 * reach, columns)
    assert 2 * reach == 8 and planes % 8 == 0 and columns % LANES == 0
    scratch = [pltpu.VMEM((views, planes, columns), jnp.float32)]

    entries = []

    def entry(level, channel, apart, direction):
        entries.append((level, channel, apart, direction))
        return len(entries) - 1

    forward_entries, back_entries = {}, {}
    for levels in groups:
        low, high = levels[0], levels[-1]
        shapes = [(low, 0), (low, 1)]
        if len(levels) == 2:
            shapes = [(low, 0), (low, 1 << high), (high, 0)]
            backs = [(high, 0), (high, 1 << low), (low, 0)]
        else:
            shapes = backs = [(low, 0)]
        forward_entries[levels] = [
            [entry(level, channel, apart, 1) for channel in (0, 1)] for level, apart in shapes
        ]
        back_entries[levels] = [
            [entry(level, channel, apart ^ (channel << level), -1) for channel in (0, 1)]
            for level, apart in backs
        ]
    tables = call(
        functools.partial(table_kernel, entries, views),
        [
            shaped(len(entries) * views * 2, LANES, dtype=jnp.int32),
            shaped(len(entries) * views * taps, LANES),
            shaped(views * crossed, LANES),
        ],
        jnp.swapaxes(interp_weight, 2, 3),
        shift_offset,
        source_view,
        cone_weight,
        specs=[SCALARS] * 4,
        name="tables",
    )
    *tables, cone = tables

    def one(index, direction, given, base=None):
        return call(
            functools.partial(part_kernel, index, direction, base is not None),
            whole,
            *tables,
            given,
            *(() if base is None else (base,)),
            name="part",
        )

    def two(first, second, direction, given, base, other):
        return call(
            functools.partial(two_kernel, first, second, direction),
            whole,
            *tables,
            given,
            base,
            other,
            scratch=scratch,
            name="two_parts",
        )

    def pair_group(steps, direction, state, first, second, third, base=None):
        near, far, joined = steps
        near_sum = one(near[0], direction, state)
        near_sum = one(near[1], direction, first, near_sum)
        far_sum = one(far[0], direction, second)
        joined_sum = one(joined[0], direction, near_sum, base)
        return two(far[1], joined[1], direction, third, far_sum, joined_sum)

    state = leaf_coeffs
    for levels in groups:
        steps = forward_entries[levels]
        near = 1 << levels[0]
        if len(levels) == 2:
            far = 1 << levels[1]
            received = [across_view(state, apart) for apart in (near, far, near + far)]
            state = pair_group(steps, 1, state, *received)
        else:
            received = across_view(state, near)
            begun = one(steps[0][0], 1, state)
            if levels != groups[-1]:
                state = one(steps[0][1], 1, received, begun)
            else:
                state, to_pair, to_across = call(
                    functools.partial(edges_kernel, reach, steps[0][1]),
                    [whole, message, message],
                    *tables,
                    received,
                    begun,
                    measured,
                    ray_weight,
                    name="edges",
                )

    from_across = across_pairs(to_across)
    from_pair = with_pair(to_pair)
    residual, cotangent = call(
        tilt_kernel,
        [whole, whole],
        cone,
        state,
        from_pair,
        from_across,
        measured,
        ray_weight,
        scratch=[
            pltpu.VMEM((views, columns // LANES, planes + beyond * reach, LANES), jnp.float32)
            for beyond in (4, 4, 4, 2)
        ],
        name="tilt",
    )

    residual = call(copy_kernel, whole, residual, name="residual")

    state = cotangent
    for levels in reversed(groups):
        steps = back_entries[levels]
        near = 1 << levels[0]
        base = leaf_coeffs if levels == groups[0] else None
        if len(levels) == 2:
            far = 1 << levels[1]
            received = [across_view(state, apart) for apart in (far, near, near + far)]
            state = pair_group(steps, -1, state, *received, base)
        else:
            received = across_view(state, near)
            begun = one(steps[0][0], -1, state, base)
            state = one(steps[0][1], -1, received, begun)
    return (residual, state)


def solution(mesh):
    in_specs = (
        P("view", "slab", None),
        P("view", "slab", None),
        P("view", "slab", None),
        P("view", None),
        P(),
        P(),
        P(),
    )
    out_specs = (P("view", "slab", None), P("view", "slab", None))
    return jax.shard_map(body, mesh=mesh, in_specs=in_specs, out_specs=out_specs, check_vma=False)
```

```python
import functools

import jax
import jax.numpy as jnp
from jax import lax
from jax.experimental import pallas as pl
from jax.experimental.pallas import tpu as pltpu
from jax.sharding import PartitionSpec as P

LANES = 128
BLOCK = pl.BlockSpec(memory_space=pltpu.VMEM)
SMALL = pltpu.CompilerParams(vmem_limit_bytes=8 << 20)


def shifted_sum(rows, moves, weights, total):
    planes, columns = rows.shape
    count = columns // LANES
    tiles = [rows[:, LANES * j : LANES * (j + 1)] for j in range(count)]
    lane = lax.broadcasted_iota(jnp.int32, (planes, LANES), 1)
    nothing = jnp.zeros((planes, LANES), jnp.float32)
    for move, weight in zip(moves, weights):
        turned = [pltpu.roll(tile, (LANES - move) & (LANES - 1), 1) for tile in tiles]
        below = lane + move < 0
        above = lane + move >= LANES
        for j in range(count):
            left = turned[j - 1] if j > 0 else nothing
            right = turned[j + 1] if j + 1 < count else nothing
            term = weight * jnp.where(below, left, jnp.where(above, right, turned[j]))
            total[j] = term if total[j] is None else total[j] + term
    return total


def table_kernel(entries, views, packed, whole_numbers, weights):
    me = lax.axis_index("view")
    kinds, rows = packed.shape[2:]
    taps = kinds - 2
    lane = lax.broadcasted_iota(jnp.int32, (kinds, rows), 1)
    for index, (level, channel, apart, direction) in enumerate(entries):
        block = packed[level, channel]
        for v in range(views):
            at = index * views + v
            chosen = jnp.sum(
                jnp.where(lane == (me ^ apart) * views + v, block, 0.0), axis=1, keepdims=True
            )
            numbers = chosen[taps:].astype(jnp.int32)
            whole_numbers[2 * at, :] = jnp.broadcast_to(numbers[0] * direction, (LANES,))
            whole_numbers[2 * at + 1, :] = jnp.broadcast_to(numbers[1], (LANES,))
            weights[pl.ds(at * taps, taps), :] = jnp.broadcast_to(chosen[:taps], (taps, LANES))


def level_part(index, direction, whole_numbers, weights, given, base, out):
    views, planes, columns = given.shape
    taps = weights.shape[0] // (whole_numbers.shape[0] // 2)
    count = columns // LANES
    if direction < 0:
        out[...] = jnp.zeros(out.shape, jnp.float32) if base is None else base[...]
    for v in range(views):
        at = index * views + v
        begin, source = whole_numbers[2 * at, 0], whole_numbers[2 * at + 1, 0]
        moves = [begin + direction * k for k in range(taps)]
        factors = [
            jnp.broadcast_to(weights[pl.ds(at * taps + k, 1), :], (planes, LANES))
            for k in range(taps)
        ]
        if direction > 0:
            total = [None] * count
            if base is not None:
                total = [base[v, :, LANES * j : LANES * (j + 1)] for j in range(count)]
            total = shifted_sum(given[source], moves, factors, total)
            for j in range(count):
                out[v, :, LANES * j : LANES * (j + 1)] = total[j]
        else:
            total = shifted_sum(given[v], moves, factors, [None] * count)
            out[source] = out[source] + jnp.concatenate(total, axis=1)


def part_kernel(index, direction, first, whole_numbers, weights, given, *refs):
    out = refs[-1]
    base = refs[0].at[:, pl.ds(first, out.shape[1])] if len(refs) == 2 else None
    level_part(index, direction, whole_numbers, weights, given, base, out)


def own_kernel(index, whole_numbers, weights, given, out, kept):
    level_part(index, 1, whole_numbers, weights, given, None, out)
    kept[...] = given[...]


def two_kernel(first, second, direction, whole_numbers, weights, given, base, other, out, between):
    level_part(first, direction, whole_numbers, weights, given, base, between)
    level_part(second, direction, whole_numbers, weights, between, other, out)


def halves_kernel(state, facing, rest):
    planes, width = state.shape[1], facing.shape[1]
    odd = lax.axis_index("slab") % 2
    facing[...] = state[:, pl.ds(pl.multiple_of(odd * (planes - width), width), width), :]
    rest[...] = state[:, pl.ds(pl.multiple_of((1 - odd) * width, width), planes - width), :]


def edge_kernel(
    reach, beyond, index, whole_numbers, weights, given, base, measured, ray, out, message
):
    level_part(index, 1, whole_numbers, weights, given, base, out)
    width = 2 * reach
    odd = lax.axis_index("slab") % 2
    top = odd if beyond else 1 - odd
    last = pl.multiple_of(top * (out.shape[1] - width), width)
    message[:, :width] = out[:, pl.ds(last, width), :]
    edge = pl.ds(pl.multiple_of(top * (measured.shape[1] - width), width), width)
    row = lax.broadcasted_iota(jnp.int32, (out.shape[0], width, out.shape[2]), 1)
    own = (row >= reach) == (top == 1)
    message[:, width:] = jnp.where(own, measured[:, edge], pltpu.roll(ray[:, edge], reach, 1))


def tilt_kernel(
    cone, rest, facing, pair, across, measured, ray, residual, cotangent, wide, seen, lengths, weighted
):
    views, planes, columns = measured.shape
    width = facing.shape[1]
    reach = width // 2
    crossed = cone.shape[0] // views
    slab = lax.axis_index("slab")
    odd = slab % 2
    at_end = (slab == 0) | (slab == lax.axis_size("slab") - 1)
    far = planes + width
    extended = planes + 2 * reach
    own = pl.ds(width, planes)
    at_facing = pl.ds(pl.multiple_of(width + odd * (planes - width), width), width)
    at_rest = pl.ds(pl.multiple_of(width + (1 - odd) * width, width), planes - width)
    for v in range(views):
        factors = [cone[pl.ds(v * crossed + e, 1), :] for e in range(crossed)]
        for j in range(columns // LANES):
            at = pl.ds(LANES * j, LANES)
            wide[v, j, at_facing] = facing[v, :, at]
            wide[v, j, at_rest] = rest[v, :, at]
            seen[v, j, own] = measured[v, :, at]
            lengths[v, j, own] = ray[v, :, at]
            for message, side, outside in ((pair, 1 - odd, False), (across, odd, at_end)):
                edge = pl.ds(pl.multiple_of(side * far, width), width)
                mixed = jnp.where(outside, 0.0, message[v, width:, at])
                wide[v, j, edge] = jnp.where(outside, 0.0, message[v, :width, at])
                seen[v, j, edge] = mixed
                lengths[v, j, edge] = pltpu.roll(mixed, reach, 0)
            total = factors[0] * wide[v, j, pl.ds(0, extended)]
            for e in range(1, crossed):
                total = total + factors[e] * wide[v, j, pl.ds(e, extended)]
            left = seen[v, j, pl.ds(reach, extended)] - total
            weighted[v, j] = lengths[v, j, pl.ds(reach, extended)] * left
            residual[v, :, at] = left[reach : reach + planes]
            total = factors[0] * weighted[v, j, pl.ds(2 * reach, planes)]
            for e in range(1, crossed):
                total = total + factors[e] * weighted[v, j, pl.ds(2 * reach - e, planes)]
            cotangent[v, :, at] = total


def copy_kernel(given, out):
    out[...] = given[...]


def shaped(*shape, dtype=jnp.float32):
    return jax.ShapeDtypeStruct(shape, dtype)


def call(kernel, out_shape, *args, scratch=(), name):
    return pl.pallas_call(
        kernel,
        out_shape=out_shape,
        in_specs=[BLOCK] * len(args),
        out_specs=jax.tree.map(lambda _: BLOCK, out_shape),
        scratch_shapes=scratch,
        compiler_params=SMALL,
        name=name,
    )(*args)


def across_view(x, apart):
    return lax.ppermute(x, "view", [(i, i ^ apart) for i in range(lax.axis_size("view"))])


def with_pair(x):
    return lax.ppermute(x, "slab", [(i, i ^ 1) for i in range(lax.axis_size("slab"))])


def across_pairs(x):
    views, count = lax.axis_size("view"), lax.axis_size("slab")
    moves = []
    for v in range(views):
        for i in range(count):
            beyond = i + 1 if i % 2 else i - 1
            to = (v, beyond) if 0 <= beyond < count else (v ^ 1, i)
            moves.append((v * count + i, to[0] * count + to[1]))
    return lax.ppermute(x, ("view", "slab"), moves)


def body(leaf_coeffs, measured, ray_weight, cone_weight, interp_weight, shift_offset, source_view):
    views, planes, columns = leaf_coeffs.shape
    crossed = cone_weight.shape[1]
    reach = crossed // 2
    taps = interp_weight.shape[3]
    level_count = lax.axis_size("view").bit_length() - 1
    groups = [(i, i + 1) for i in range(0, level_count - 2, 2)]
    groups += [(i,) for i in range(2 * len(groups), level_count)]
    whole = shaped(views, planes, columns)
    message = shaped(views, 4 * reach, columns)
    assert 2 * reach == 8 and planes % 16 == 0 and columns % LANES == 0

    entries = []

    def entry(level, channel, apart, direction):
        entries.append((level, channel, apart, direction))
        return len(entries) - 1

    forward_entries, back_entries = {}, {}
    for levels in groups:
        low, high = levels[0], levels[-1]
        shapes = [(low, 0), (low, 1)]
        if len(levels) == 2:
            shapes = [(low, 0), (low, 1 << high), (high, 0)]
            backs = [(high, 0), (high, 1 << low), (low, 0)]
        else:
            shapes = backs = [(low, 0)]
        forward_entries[levels] = [
            [entry(level, channel, apart, 1) for channel in (0, 1)] for level, apart in shapes
        ]
        back_entries[levels] = [
            [entry(level, channel, apart ^ (channel << level), -1) for channel in (0, 1)]
            for level, apart in backs
        ]
    packed = jnp.concatenate(
        [jnp.swapaxes(interp_weight, 2, 3)]
        + [x[:, :, None].astype(jnp.float32) for x in (shift_offset, source_view)],
        axis=2,
    )
    tables = call(
        functools.partial(table_kernel, entries, views),
        [
            shaped(len(entries) * views * 2, LANES, dtype=jnp.int32),
            shaped(len(entries) * views * taps, LANES),
        ],
        packed,
        name="tables",
    )
    cone = jnp.broadcast_to(cone_weight.reshape(-1, 1), (views * crossed, LANES))

    def one(index, direction, given, base=None, first=0):
        return call(
            functools.partial(part_kernel, index, direction, first),
            shaped(*given.shape),
            *tables,
            given,
            *(() if base is None else (base,)),
            name="part",
        )

    def two(first, second, direction, given, base, other):
        return call(
            functools.partial(two_kernel, first, second, direction),
            shaped(*given.shape),
            *tables,
            given,
            base,
            other,
            scratch=[pltpu.VMEM(given.shape, jnp.float32)],
            name="two_parts",
        )

    kept = [leaf_coeffs]

    def begin(index, direction, state):
        if state is not leaf_coeffs:
            return one(index, direction, state)
        own, kept[0] = call(
            functools.partial(own_kernel, index), [whole, whole], *tables, state, name="own"
        )
        return own

    def forward_pair(steps, direction, state, first, second, third, base=None):
        own_steps, other_steps, joined = steps
        other = one(other_steps[1], direction, third)
        other = one(other_steps[0], direction, second, other)
        joined_sum = one(joined[1], direction, other, base)
        own = begin(own_steps[0], direction, state)
        return two(own_steps[1], joined[0], direction, first, own, joined_sum)

    def back_pair(steps, direction, state, first, second, third, base=None):
        own_steps, other_steps, joined = steps
        other = one(other_steps[1], direction, third)
        other = one(other_steps[0], direction, second, other)
        joined_sum = one(joined[1], direction, other, base)
        own = begin(own_steps[0], direction, state)
        return two(own_steps[1], joined[0], direction, first, own, joined_sum)

    state = leaf_coeffs
    for levels in groups[:-1]:
        steps = forward_entries[levels]
        near = 1 << levels[0]
        if len(levels) == 2:
            far = 1 << levels[1]
            received = [across_view(state, apart) for apart in (near, far, near + far)]
            state = forward_pair(steps, 1, state, *received)
        else:
            received = across_view(state, near)
            state = one(steps[0][1], 1, received, one(steps[0][0], 1, state))

    own_step, partner_step = forward_entries[groups[-1]][0]
    width = 2 * reach
    halves = call(
        halves_kernel,
        [shaped(views, width, columns), shaped(views, planes - width, columns)],
        state,
        name="halves",
    )
    halves = halves[::-1]
    received = [across_view(half, 1 << groups[-1][0]) for half in halves]
    begun = [one(own_step, 1, half) for half in halves]
    (rest, to_pair), (facing, to_across) = [
        call(
            functools.partial(edge_kernel, reach, beyond, partner_step),
            [shaped(*half.shape), message],
            *tables,
            half,
            base,
            measured,
            ray_weight,
            name="edge",
        )
        for beyond, half, base in zip((False, True), received, begun)
    ]
    from_pair = with_pair(to_pair)
    from_across = across_pairs(to_across)

    residual, cotangent = call(
        tilt_kernel,
        [whole, whole],
        cone,
        rest,
        facing,
        from_pair,
        from_across,
        measured,
        ray_weight,
        scratch=[
            pltpu.VMEM((views, columns // LANES, planes + beyond * reach, LANES), jnp.float32)
            for beyond in (4, 4, 4, 2)
        ],
        name="tilt",
    )

    residual = call(copy_kernel, whole, residual, name="residual")

    state = cotangent
    for levels in reversed(groups):
        steps = back_entries[levels]
        near = 1 << levels[0]
        base = kept[0] if levels == groups[0] else None
        if len(levels) == 2:
            far = 1 << levels[1]
            received = [across_view(state, apart) for apart in (far, near, near + far)]
            state = back_pair(steps, -1, state, *received, base)
        else:
            received = across_view(state, near)
            state = one(steps[0][1], -1, received, one(steps[0][0], -1, state, base))
    return (residual, state)


def solution(mesh):
    in_specs = (
        P("view", "slab", None),
        P("view", "slab", None),
        P("view", "slab", None),
        P("view", None),
        P(),
        P(),
        P(),
    )
    out_specs = (P("view", "slab", None), P("view", "slab", None))
    return jax.shard_map(body, mesh=mesh, in_specs=in_specs, out_specs=out_specs, check_vma=False)
```

```python
import functools

import jax
import jax.numpy as jnp
from jax import lax
from jax.experimental import pallas as pl
from jax.experimental.pallas import tpu as pltpu
from jax.sharding import PartitionSpec as P

LANES = 128
BLOCK = pl.BlockSpec(memory_space=pltpu.VMEM)
SMALL = pltpu.CompilerParams(vmem_limit_bytes=8 << 20)


def shifted_sum(rows, move, weights):
    planes, columns = rows.shape
    count = columns // LANES
    tiles = [rows[:, LANES * j : LANES * (j + 1)] for j in range(count)]
    lane = lax.broadcasted_iota(jnp.int32, (planes, LANES), 1)
    nothing = jnp.zeros((planes, LANES), jnp.float32)
    total = [None] * count
    for k, weight in enumerate(weights):
        turned = [pltpu.roll(tile, (LANES - move - k) & (LANES - 1), 1) for tile in tiles]
        below = lane + (move + k) < 0
        above = lane + (move + k) >= LANES
        for j in range(count):
            left = turned[j - 1] if j > 0 else nothing
            right = turned[j + 1] if j + 1 < count else nothing
            term = weight * jnp.where(below, left, jnp.where(above, right, turned[j]))
            total[j] = term if total[j] is None else total[j] + term
    return total


def table_kernel(entries, views, packed, whole_numbers, weights):
    me = lax.axis_index("view")
    kinds, rows = packed.shape[2:]
    taps = kinds - 2
    lane = lax.broadcasted_iota(jnp.int32, (kinds, rows), 1)
    for index, (level, channel, apart, direction) in enumerate(entries):
        block = packed[level, channel]
        for v in range(views):
            at = index * views + v
            chosen = jnp.sum(
                jnp.where(lane == (me ^ apart) * views + v, block, 0.0), axis=1, keepdims=True
            )
            numbers = chosen[taps:].astype(jnp.int32)
            whole_numbers[2 * at, :] = jnp.broadcast_to(numbers[0] * direction, (LANES,))
            whole_numbers[2 * at + 1, :] = jnp.broadcast_to(numbers[1], (LANES,))
            weights[pl.ds(at * taps, taps), :] = jnp.broadcast_to(chosen[:taps], (taps, LANES))


def level_part(index, direction, whole_numbers, weights, given, base, out):
    views, planes, columns = given.shape
    taps = weights.shape[0] // (whole_numbers.shape[0] // 2)
    count = columns // LANES
    rows = [index * views + v for v in range(views)]
    begins = [whole_numbers[2 * at, 0] for at in rows]
    sources = [whole_numbers[2 * at + 1, 0] for at in rows]
    sums = []
    for v, at in enumerate(rows):
        factors = [
            jnp.broadcast_to(weights[pl.ds(at * taps + k, 1), :], (planes, LANES))
            for k in range(taps)
        ]
        if direction > 0:
            sums.append(shifted_sum(given[sources[v]], begins[v], factors))
        else:
            sums.append(shifted_sum(given[v], begins[v] - (taps - 1), factors[::-1]))
    for m in range(views):
        for j in range(count):
            at = pl.ds(LANES * j, LANES)
            if direction > 0:
                total = sums[m][j]
            else:
                total = sum(jnp.where(sources[v] == m, sums[v][j], 0.0) for v in range(views))
            out[m, :, at] = total if base is None else base[m, :, at] + total


def part_kernel(index, direction, whole_numbers, weights, given, *refs):
    base = refs[0] if len(refs) == 2 else None
    level_part(index, direction, whole_numbers, weights, given, base, refs[-1])


def own_kernel(index, whole_numbers, weights, given, out, kept):
    level_part(index, 1, whole_numbers, weights, given, None, out)
    kept[...] = given[...]


def four_kernel(steps, direction, whole_numbers, weights, first, second, own, other, *refs):
    out, near, far, joined = refs
    level_part(steps[0], direction, whole_numbers, weights, second, other, far)
    level_part(steps[1], direction, whole_numbers, weights, first, own, near)
    level_part(steps[2], direction, whole_numbers, weights, far, None, joined)
    level_part(steps[3], direction, whole_numbers, weights, near, joined, out)


def two_kernel(first, second, direction, whole_numbers, weights, given, base, other, out, between):
    level_part(first, direction, whole_numbers, weights, given, base, between)
    level_part(second, direction, whole_numbers, weights, between, other, out)


def halves_kernel(state, facing, rest):
    planes, width = state.shape[1], facing.shape[1]
    odd = lax.axis_index("slab") % 2
    facing[...] = state[:, pl.ds(pl.multiple_of(odd * (planes - width), width), width), :]
    rest[...] = state[:, pl.ds(pl.multiple_of((1 - odd) * width, width), planes - width), :]


def edge_kernel(
    reach, beyond, index, whole_numbers, weights, given, base, measured, ray, out, message
):
    level_part(index, 1, whole_numbers, weights, given, base, out)
    width = 2 * reach
    odd = lax.axis_index("slab") % 2
    top = odd if beyond else 1 - odd
    last = pl.multiple_of(top * (out.shape[1] - width), width)
    message[:, :width] = out[:, pl.ds(last, width), :]
    edge = pl.ds(pl.multiple_of(top * (measured.shape[1] - width), width), width)
    row = lax.broadcasted_iota(jnp.int32, (out.shape[0], width, out.shape[2]), 1)
    own = (row >= reach) == (top == 1)
    message[:, width:] = jnp.where(own, measured[:, edge], pltpu.roll(ray[:, edge], reach, 1))


def tilt_kernel(
    beyond, cone, facing, rest, message, measured, ray, residual, cotangent, wide, seen, lengths, weighted
):
    views, planes, columns = measured.shape
    width = facing.shape[1]
    reach = width // 2
    crossed = cone.shape[0] // views
    slab = lax.axis_index("slab")
    odd = slab % 2
    high = odd if beyond else 1 - odd
    outside = beyond & ((slab == 0) | (slab == lax.axis_size("slab") - 1))
    begin = (1 - high) * width
    at_edge = pl.ds(pl.multiple_of(high * planes, width), width)
    at_own = pl.ds(pl.multiple_of(begin, width), planes)
    at_facing = pl.ds(pl.multiple_of(begin + odd * (planes - width), width), width)
    at_rest = pl.ds(pl.multiple_of(begin + (1 - odd) * width, width), planes - width)
    out = residual.shape[1]
    extended = out + 2 * reach
    first = pl.multiple_of(high * (planes - out - width), width)
    for v in range(views):
        factors = [cone[pl.ds(v * crossed + e, 1), :] for e in range(crossed)]
        for j in range(columns // LANES):
            at = pl.ds(LANES * j, LANES)
            mixed = jnp.where(outside, 0.0, message[v, width:, at])
            wide[v, j, at_facing] = facing[v, :, at]
            wide[v, j, at_rest] = rest[v, :, at]
            wide[v, j, at_edge] = jnp.where(outside, 0.0, message[v, :width, at])
            seen[v, j, at_own] = measured[v, :, at]
            seen[v, j, at_edge] = mixed
            lengths[v, j, at_own] = ray[v, :, at]
            lengths[v, j, at_edge] = pltpu.roll(mixed, reach, 0)
            total = factors[0] * wide[v, j, pl.ds(first, extended)]
            for e in range(1, crossed):
                total = total + factors[e] * wide[v, j, pl.ds(first + e, extended)]
            left = seen[v, j, pl.ds(first + reach, extended)] - total
            weighted[v, j] = lengths[v, j, pl.ds(first + reach, extended)] * left
            residual[v, :, at] = left[reach : reach + out]
            total = factors[0] * weighted[v, j, pl.ds(2 * reach, out)]
            for e in range(1, crossed):
                total = total + factors[e] * weighted[v, j, pl.ds(2 * reach - e, out)]
            cotangent[v, :, at] = total


def unite_kernel(facing, rest, out):
    planes, width = out.shape[1], facing.shape[1]
    odd = lax.axis_index("slab") % 2
    out[:, pl.ds(pl.multiple_of(odd * (planes - width), width), width), :] = facing[...]
    out[:, pl.ds(pl.multiple_of((1 - odd) * width, width), planes - width), :] = rest[...]


def shaped(*shape, dtype=jnp.float32):
    return jax.ShapeDtypeStruct(shape, dtype)


def call(kernel, out_shape, *args, scratch=(), name):
    return pl.pallas_call(
        kernel,
        out_shape=out_shape,
        in_specs=[BLOCK] * len(args),
        out_specs=jax.tree.map(lambda _: BLOCK, out_shape),
        scratch_shapes=scratch,
        compiler_params=SMALL,
        name=name,
    )(*args)


def across_view(x, apart):
    return lax.ppermute(x, "view", [(i, i ^ apart) for i in range(lax.axis_size("view"))])


def with_pair(x):
    return lax.ppermute(x, "slab", [(i, i ^ 1) for i in range(lax.axis_size("slab"))])


def across_pairs(x):
    views, count = lax.axis_size("view"), lax.axis_size("slab")
    moves = []
    for v in range(views):
        for i in range(count):
            beyond = i + 1 if i % 2 else i - 1
            to = (v, beyond) if 0 <= beyond < count else (v ^ 1, i)
            moves.append((v * count + i, to[0] * count + to[1]))
    return lax.ppermute(x, ("view", "slab"), moves)


def body(leaf_coeffs, measured, ray_weight, cone_weight, interp_weight, shift_offset, source_view):
    views, planes, columns = leaf_coeffs.shape
    crossed = cone_weight.shape[1]
    reach = crossed // 2
    taps = interp_weight.shape[3]
    level_count = lax.axis_size("view").bit_length() - 1
    groups = [(i, i + 1) for i in range(0, level_count - 2, 2)]
    groups += [(i,) for i in range(2 * len(groups), level_count)]
    whole = shaped(views, planes, columns)
    message = shaped(views, 4 * reach, columns)
    assert 2 * reach == 8 and planes % 16 == 0 and columns % LANES == 0

    entries = []

    def entry(level, channel, apart, direction):
        entries.append((level, channel, apart, direction))
        return len(entries) - 1

    forward_entries, back_entries = {}, {}
    for levels in groups:
        low, high = levels[0], levels[-1]
        if len(levels) == 2:
            shapes = [(low, 0), (low, 1 << high), (high, 0)]
            backs = [(high, 0), (high, 1 << low), (low, 0)]
        else:
            shapes = backs = [(low, 0)]
        forward_entries[levels] = [
            [entry(level, channel, apart, 1) for channel in (0, 1)] for level, apart in shapes
        ]
        back_entries[levels] = [
            [entry(level, channel, apart ^ (channel << level), -1) for channel in (0, 1)]
            for level, apart in backs
        ]
    packed = jnp.concatenate(
        [jnp.swapaxes(interp_weight, 2, 3)]
        + [x[:, :, None].astype(jnp.float32) for x in (shift_offset, source_view)],
        axis=2,
    )
    tables = call(
        functools.partial(table_kernel, entries, views),
        [
            shaped(len(entries) * views * 2, LANES, dtype=jnp.int32),
            shaped(len(entries) * views * taps, LANES),
        ],
        packed,
        name="tables",
    )
    cone = jnp.broadcast_to(cone_weight.reshape(-1, 1), (views * crossed, LANES))

    def one(index, direction, given, base=None):
        return call(
            functools.partial(part_kernel, index, direction),
            shaped(*given.shape),
            *tables,
            given,
            *(() if base is None else (base,)),
            name="part",
        )

    def two(first, second, direction, given, base, other):
        return call(
            functools.partial(two_kernel, first, second, direction),
            shaped(*given.shape),
            *tables,
            given,
            base,
            other,
            scratch=[pltpu.VMEM(given.shape, jnp.float32)],
            name="two_parts",
        )

    kept = [leaf_coeffs]

    def begin(index, direction, state):
        if state is not leaf_coeffs:
            return one(index, direction, state)
        own, kept[0] = call(
            functools.partial(own_kernel, index), [whole, whole], *tables, state, name="own"
        )
        return own

    def forward_pair(steps, direction, state, first, second, third):
        own_steps, other_steps, joined = steps
        other = one(other_steps[1], direction, third)
        own = begin(own_steps[0], direction, state)
        numbers = (other_steps[0], own_steps[1], joined[1], joined[0])
        return call(
            functools.partial(four_kernel, numbers, direction),
            shaped(*state.shape),
            *tables,
            first,
            second,
            own,
            other,
            scratch=[pltpu.VMEM(state.shape, jnp.float32)] * 3,
            name="four_parts",
        )

    def back_pair(steps, direction, state, first, second, third, base=None):
        own_steps, other_steps, joined = steps
        other = one(other_steps[1], direction, third)
        other = one(other_steps[0], direction, second, other)
        joined_sum = one(joined[1], direction, other, base)
        own = begin(own_steps[0], direction, state)
        return two(own_steps[1], joined[0], direction, first, own, joined_sum)

    state = leaf_coeffs
    for levels in groups[:-1]:
        steps = forward_entries[levels]
        near = 1 << levels[0]
        if len(levels) == 2:
            far = 1 << levels[1]
            received = [across_view(state, apart) for apart in (near, far, near + far)]
            state = forward_pair(steps, 1, state, *received)
        else:
            received = across_view(state, near)
            state = one(steps[0][1], 1, received, one(steps[0][0], 1, state))

    own_step, partner_step = forward_entries[groups[-1]][0]
    width = 2 * reach
    halves = call(
        halves_kernel,
        [shaped(views, width, columns), shaped(views, planes - width, columns)],
        state,
        name="halves",
    )
    halves = halves[::-1]
    received = [across_view(half, 1 << groups[-1][0]) for half in halves]
    begun = [one(own_step, 1, half) for half in halves]
    (rest, to_pair), (facing, to_across) = [
        call(
            functools.partial(edge_kernel, reach, beyond, partner_step),
            [shaped(*half.shape), message],
            *tables,
            half,
            base,
            measured,
            ray_weight,
            name="edge",
        )
        for beyond, half, base in zip((False, True), received, begun)
    ]
    from_pair = with_pair(to_pair)
    from_across = across_pairs(to_across)

    def tilt(beyond, received, like):
        return call(
            functools.partial(tilt_kernel, beyond),
            [shaped(*like.shape)] * 2,
            cone,
            facing,
            rest,
            received,
            measured,
            ray_weight,
            scratch=[
                pltpu.VMEM((views, columns // LANES, rows, LANES), jnp.float32)
                for rows in [planes + width] * 3 + [like.shape[1] + width]
            ],
            name="tilt",
        )

    last = groups[-1][0]
    own_step, partner_step = back_entries[groups[-1]][0]
    residuals, sums = [], []
    for beyond, received, like in ((False, from_pair, rest), (True, from_across, facing)):
        residual, cotangent = tilt(beyond, received, like)
        received = across_view(cotangent, 1 << last)
        begun = one(own_step, -1, cotangent)
        residuals.insert(0, residual)
        sums.insert(0, one(partner_step, -1, received, begun))
    residual = call(unite_kernel, whole, *residuals, name="residual")
    state = call(unite_kernel, whole, *sums, name="unite")
    for levels in reversed(groups[:-1]):
        steps = back_entries[levels]
        near = 1 << levels[0]
        base = kept[0] if levels == groups[0] else None
        if len(levels) == 2:
            far = 1 << levels[1]
            received = [across_view(state, apart) for apart in (far, near, near + far)]
            state = back_pair(steps, -1, state, *received, base)
        else:
            received = across_view(state, near)
            state = one(steps[0][1], -1, received, one(steps[0][0], -1, state, base))
    return (residual, state)


def solution(mesh):
    in_specs = (
        P("view", "slab", None),
        P("view", "slab", None),
        P("view", "slab", None),
        P("view", None),
        P(),
        P(),
        P(),
    )
    out_specs = (P("view", "slab", None), P("view", "slab", None))
    return jax.shard_map(body, mesh=mesh, in_specs=in_specs, out_specs=out_specs, check_vma=False)
```

```python
import functools

import jax
import jax.numpy as jnp
from jax import lax
from jax.experimental import pallas as pl
from jax.experimental.pallas import tpu as pltpu
from jax.sharding import PartitionSpec as P

LANES = 128
BLOCK = pl.BlockSpec(memory_space=pltpu.VMEM)
SMALL = pltpu.CompilerParams(vmem_limit_bytes=8 << 20)


def shifted_sum(rows, moves, weights, total):
    planes, columns = rows.shape
    count = columns // LANES
    tiles = [rows[:, LANES * j : LANES * (j + 1)] for j in range(count)]
    lane = lax.broadcasted_iota(jnp.int32, (planes, LANES), 1)
    nothing = jnp.zeros((planes, LANES), jnp.float32)
    for move, weight in zip(moves, weights):
        turned = [pltpu.roll(tile, (LANES - move) & (LANES - 1), 1) for tile in tiles]
        below = lane + move < 0
        above = lane + move >= LANES
        for j in range(count):
            left = turned[j - 1] if j > 0 else nothing
            right = turned[j + 1] if j + 1 < count else nothing
            term = weight * jnp.where(below, left, jnp.where(above, right, turned[j]))
            total[j] = term if total[j] is None else total[j] + term
    return total


def table_kernel(entries, views, packed, whole_numbers, weights):
    me = lax.axis_index("view")
    kinds, rows = packed.shape[2:]
    taps = kinds - 2
    lane = lax.broadcasted_iota(jnp.int32, (kinds, rows), 1)
    for index, (level, channel, apart, direction) in enumerate(entries):
        block = packed[level, channel]
        for v in range(views):
            at = index * views + v
            chosen = jnp.sum(
                jnp.where(lane == (me ^ apart) * views + v, block, 0.0), axis=1, keepdims=True
            )
            numbers = chosen[taps:].astype(jnp.int32)
            whole_numbers[2 * at, :] = jnp.broadcast_to(numbers[0] * direction, (LANES,))
            whole_numbers[2 * at + 1, :] = jnp.broadcast_to(numbers[1], (LANES,))
            weights[pl.ds(at * taps, taps), :] = jnp.broadcast_to(chosen[:taps], (taps, LANES))


def level_part(index, direction, whole_numbers, weights, given, base, out):
    views, planes, columns = given.shape
    taps = weights.shape[0] // (whole_numbers.shape[0] // 2)
    count = columns // LANES
    if direction < 0:
        out[...] = jnp.zeros(out.shape, jnp.float32) if base is None else base[...]
    for v in range(views):
        at = index * views + v
        begin, source = whole_numbers[2 * at, 0], whole_numbers[2 * at + 1, 0]
        moves = [begin + direction * k for k in range(taps)]
        factors = [
            jnp.broadcast_to(weights[pl.ds(at * taps + k, 1), :], (planes, LANES))
            for k in range(taps)
        ]
        if direction > 0:
            total = [None] * count
            if base is not None:
                total = [base[v, :, LANES * j : LANES * (j + 1)] for j in range(count)]
            total = shifted_sum(given[source], moves, factors, total)
            for j in range(count):
                out[v, :, LANES * j : LANES * (j + 1)] = total[j]
        else:
            total = shifted_sum(given[v], moves, factors, [None] * count)
            out[source] = out[source] + jnp.concatenate(total, axis=1)


def part_kernel(index, direction, first, whole_numbers, weights, given, *refs):
    out = refs[-1]
    base = refs[0].at[:, pl.ds(first, out.shape[1])] if len(refs) == 2 else None
    level_part(index, direction, whole_numbers, weights, given, base, out)


def own_kernel(index, whole_numbers, weights, given, out, kept):
    level_part(index, 1, whole_numbers, weights, given, None, out)
    kept[...] = given[...]


def two_kernel(first, second, direction, whole_numbers, weights, given, base, other, out, between):
    level_part(first, direction, whole_numbers, weights, given, base, between)
    level_part(second, direction, whole_numbers, weights, between, other, out)


def halves_kernel(state, facing, rest):
    planes, width = state.shape[1], facing.shape[1]
    odd = lax.axis_index("slab") % 2
    facing[...] = state[:, pl.ds(pl.multiple_of(odd * (planes - width), width), width), :]
    rest[...] = state[:, pl.ds(pl.multiple_of((1 - odd) * width, width), planes - width), :]


def mix_kernel(reach, measured, ray, token, pair, across):
    width = 2 * reach
    odd = lax.axis_index("slab") % 2
    row = lax.broadcasted_iota(jnp.int32, pair.shape, 1)
    for mixed, top in ((pair, 1 - odd), (across, odd)):
        edge = pl.ds(pl.multiple_of(top * (measured.shape[1] - width), width), width)
        own = (row >= reach) == (top == 1)
        mixed[...] = jnp.where(own, measured[:, edge], pltpu.roll(ray[:, edge], reach, 1))


def edge_kernel(reach, beyond, index, whole_numbers, weights, given, base, out, message):
    level_part(index, 1, whole_numbers, weights, given, base, out)
    width = 2 * reach
    odd = lax.axis_index("slab") % 2
    top = odd if beyond else 1 - odd
    last = pl.multiple_of(top * (out.shape[1] - width), width)
    message[...] = out[:, pl.ds(last, width), :]


def tilt_kernel(
    cone, rest, facing, pair, across, pair_mix, across_mix, measured, ray, residual, cotangent, wide, seen, lengths, weighted
):
    views, planes, columns = measured.shape
    width = facing.shape[1]
    reach = width // 2
    crossed = cone.shape[0] // views
    slab = lax.axis_index("slab")
    odd = slab % 2
    at_end = (slab == 0) | (slab == lax.axis_size("slab") - 1)
    far = planes + width
    extended = planes + 2 * reach
    own = pl.ds(width, planes)
    at_facing = pl.ds(pl.multiple_of(width + odd * (planes - width), width), width)
    at_rest = pl.ds(pl.multiple_of(width + (1 - odd) * width, width), planes - width)
    for v in range(views):
        factors = [cone[pl.ds(v * crossed + e, 1), :] for e in range(crossed)]
        for j in range(columns // LANES):
            at = pl.ds(LANES * j, LANES)
            wide[v, j, at_facing] = facing[v, :, at]
            wide[v, j, at_rest] = rest[v, :, at]
            seen[v, j, own] = measured[v, :, at]
            lengths[v, j, own] = ray[v, :, at]
            for message, mixture, side, outside in (
                (pair, pair_mix, 1 - odd, False),
                (across, across_mix, odd, at_end),
            ):
                edge = pl.ds(pl.multiple_of(side * far, width), width)
                mixed = jnp.where(outside, 0.0, mixture[v, :, at])
                wide[v, j, edge] = jnp.where(outside, 0.0, message[v, :, at])
                seen[v, j, edge] = mixed
                lengths[v, j, edge] = pltpu.roll(mixed, reach, 0)
            total = factors[0] * wide[v, j, pl.ds(0, extended)]
            for e in range(1, crossed):
                total = total + factors[e] * wide[v, j, pl.ds(e, extended)]
            left = seen[v, j, pl.ds(reach, extended)] - total
            weighted[v, j] = lengths[v, j, pl.ds(reach, extended)] * left
            residual[v, :, at] = left[reach : reach + planes]
            total = factors[0] * weighted[v, j, pl.ds(2 * reach, planes)]
            for e in range(1, crossed):
                total = total + factors[e] * weighted[v, j, pl.ds(2 * reach - e, planes)]
            cotangent[v, :, at] = total


def copy_kernel(given, out):
    out[...] = given[...]


def shaped(*shape, dtype=jnp.float32):
    return jax.ShapeDtypeStruct(shape, dtype)


def call(kernel, out_shape, *args, scratch=(), name):
    return pl.pallas_call(
        kernel,
        out_shape=out_shape,
        in_specs=[BLOCK] * len(args),
        out_specs=jax.tree.map(lambda _: BLOCK, out_shape),
        scratch_shapes=scratch,
        compiler_params=SMALL,
        name=name,
    )(*args)


def across_view(x, apart):
    return lax.ppermute(x, "view", [(i, i ^ apart) for i in range(lax.axis_size("view"))])


def with_pair(x):
    return lax.ppermute(x, "slab", [(i, i ^ 1) for i in range(lax.axis_size("slab"))])


def across_pairs(x):
    views, count = lax.axis_size("view"), lax.axis_size("slab")
    moves = []
    for v in range(views):
        for i in range(count):
            beyond = i + 1 if i % 2 else i - 1
            to = (v, beyond) if 0 <= beyond < count else (v ^ 1, i)
            moves.append((v * count + i, to[0] * count + to[1]))
    return lax.ppermute(x, ("view", "slab"), moves)


def body(leaf_coeffs, measured, ray_weight, cone_weight, interp_weight, shift_offset, source_view):
    views, planes, columns = leaf_coeffs.shape
    crossed = cone_weight.shape[1]
    reach = crossed // 2
    taps = interp_weight.shape[3]
    level_count = lax.axis_size("view").bit_length() - 1
    groups = [(i, i + 1) for i in range(0, level_count - 2, 2)]
    groups += [(i,) for i in range(2 * len(groups), level_count)]
    whole = shaped(views, planes, columns)
    message = shaped(views, 2 * reach, columns)
    assert 2 * reach == 8 and planes % 16 == 0 and columns % LANES == 0

    entries = []

    def entry(level, channel, apart, direction):
        entries.append((level, channel, apart, direction))
        return len(entries) - 1

    forward_entries, back_entries = {}, {}
    for levels in groups:
        low, high = levels[0], levels[-1]
        shapes = [(low, 0), (low, 1)]
        if len(levels) == 2:
            shapes = [(low, 0), (low, 1 << high), (high, 0)]
            backs = [(high, 0), (high, 1 << low), (low, 0)]
        else:
            shapes = backs = [(low, 0)]
        forward_entries[levels] = [
            [entry(level, channel, apart, 1) for channel in (0, 1)] for level, apart in shapes
        ]
        back_entries[levels] = [
            [entry(level, channel, apart ^ (channel << level), -1) for channel in (0, 1)]
            for level, apart in backs
        ]
    packed = jnp.concatenate(
        [jnp.swapaxes(interp_weight, 2, 3)]
        + [x[:, :, None].astype(jnp.float32) for x in (shift_offset, source_view)],
        axis=2,
    )
    tables = call(
        functools.partial(table_kernel, entries, views),
        [
            shaped(len(entries) * views * 2, LANES, dtype=jnp.int32),
            shaped(len(entries) * views * taps, LANES),
        ],
        packed,
        name="tables",
    )
    cone = jnp.broadcast_to(cone_weight.reshape(-1, 1), (views * crossed, LANES))

    def one(index, direction, given, base=None, first=0):
        return call(
            functools.partial(part_kernel, index, direction, first),
            shaped(*given.shape),
            *tables,
            given,
            *(() if base is None else (base,)),
            name="part",
        )

    def two(first, second, direction, given, base, other):
        return call(
            functools.partial(two_kernel, first, second, direction),
            shaped(*given.shape),
            *tables,
            given,
            base,
            other,
            scratch=[pltpu.VMEM(given.shape, jnp.float32)],
            name="two_parts",
        )

    kept = [leaf_coeffs]

    def begin(index, direction, state):
        if state is not leaf_coeffs:
            return one(index, direction, state)
        own, kept[0] = call(
            functools.partial(own_kernel, index), [whole, whole], *tables, state, name="own"
        )
        return own

    def forward_pair(steps, direction, state, first, second, third, base=None):
        own_steps, other_steps, joined = steps
        other = one(other_steps[1], direction, third)
        other = one(other_steps[0], direction, second, other)
        joined_sum = one(joined[1], direction, other, base)
        own = begin(own_steps[0], direction, state)
        return two(own_steps[1], joined[0], direction, first, own, joined_sum)

    def back_pair(steps, direction, state, first, second, third, base=None):
        own_steps, other_steps, joined = steps
        other = one(other_steps[1], direction, third)
        other = one(other_steps[0], direction, second, other)
        joined_sum = one(joined[1], direction, other, base)
        own = begin(own_steps[0], direction, state)
        return two(own_steps[1], joined[0], direction, first, own, joined_sum)

    state = leaf_coeffs
    for levels in groups[:-1]:
        steps = forward_entries[levels]
        near = 1 << levels[0]
        if len(levels) == 2:
            far = 1 << levels[1]
            received = [across_view(state, apart) for apart in (near, far, near + far)]
            state = forward_pair(steps, 1, state, *received)
        else:
            received = across_view(state, near)
            state = one(steps[0][1], 1, received, one(steps[0][0], 1, state))

    pair_mix, across_mix = call(
        functools.partial(mix_kernel, reach),
        [message, message],
        measured,
        ray_weight,
        kept[0],
        name="mix",
    )
    pair_mix, across_mix = with_pair(pair_mix), across_pairs(across_mix)

    own_step, partner_step = forward_entries[groups[-1]][0]
    width = 2 * reach
    halves = call(
        halves_kernel,
        [shaped(views, width, columns), shaped(views, planes - width, columns)],
        state,
        name="halves",
    )
    halves = halves[::-1]
    received = [across_view(half, 1 << groups[-1][0]) for half in halves]
    begun = [one(own_step, 1, half) for half in halves]
    (rest, to_pair), (facing, to_across) = [
        call(
            functools.partial(edge_kernel, reach, beyond, partner_step),
            [shaped(*half.shape), message],
            *tables,
            half,
            base,
            name="edge",
        )
        for beyond, half, base in zip((False, True), received, begun)
    ]
    from_pair = with_pair(to_pair)
    from_across = across_pairs(to_across)

    residual, cotangent = call(
        tilt_kernel,
        [whole, whole],
        cone,
        rest,
        facing,
        from_pair,
        from_across,
        pair_mix,
        across_mix,
        measured,
        ray_weight,
        scratch=[
            pltpu.VMEM((views, columns // LANES, planes + beyond * reach, LANES), jnp.float32)
            for beyond in (4, 4, 4, 2)
        ],
        name="tilt",
    )

    residual = call(copy_kernel, whole, residual, name="residual")

    state = cotangent
    for levels in reversed(groups):
        steps = back_entries[levels]
        near = 1 << levels[0]
        base = kept[0] if levels == groups[0] else None
        if len(levels) == 2:
            far = 1 << levels[1]
            received = [across_view(state, apart) for apart in (far, near, near + far)]
            state = back_pair(steps, -1, state, *received, base)
        else:
            received = across_view(state, near)
            state = one(steps[0][1], -1, received, one(steps[0][0], -1, state, base))
    return (residual, state)


def solution(mesh):
    in_specs = (
        P("view", "slab", None),
        P("view", "slab", None),
        P("view", "slab", None),
        P("view", None),
        P(),
        P(),
        P(),
    )
    out_specs = (P("view", "slab", None), P("view", "slab", None))
    return jax.shard_map(body, mesh=mesh, in_specs=in_specs, out_specs=out_specs, check_vma=False)
```

```python
import functools

import jax
import jax.numpy as jnp
from jax import lax
from jax.experimental import pallas as pl
from jax.experimental.pallas import tpu as pltpu
from jax.sharding import PartitionSpec as P

LANES = 128
BLOCK = pl.BlockSpec(memory_space=pltpu.VMEM)
SMALL = pltpu.CompilerParams(vmem_limit_bytes=8 << 20)


def shifted_sum(rows, move, weights):
    planes, columns = rows.shape
    count = columns // LANES
    tiles = [rows[:, LANES * j : LANES * (j + 1)] for j in range(count)]
    lane = lax.broadcasted_iota(jnp.int32, (planes, LANES), 1)
    nothing = jnp.zeros((planes, LANES), jnp.float32)
    total = [None] * count
    for k, weight in enumerate(weights):
        turned = [pltpu.roll(tile, (LANES - move - k) & (LANES - 1), 1) for tile in tiles]
        below = lane + (move + k) < 0
        above = lane + (move + k) >= LANES
        for j in range(count):
            left = turned[j - 1] if j > 0 else nothing
            right = turned[j + 1] if j + 1 < count else nothing
            term = weight * jnp.where(below, left, jnp.where(above, right, turned[j]))
            total[j] = term if total[j] is None else total[j] + term
    return total


def table_kernel(entries, views, packed, whole_numbers, weights):
    me = lax.axis_index("view")
    kinds, rows = packed.shape[2:]
    taps = kinds - 2
    lane = lax.broadcasted_iota(jnp.int32, (kinds, rows), 1)
    for index, (level, channel, apart, direction) in enumerate(entries):
        block = packed[level, channel]
        for v in range(views):
            at = index * views + v
            chosen = jnp.sum(
                jnp.where(lane == (me ^ apart) * views + v, block, 0.0), axis=1, keepdims=True
            )
            numbers = chosen[taps:].astype(jnp.int32)
            whole_numbers[2 * at, :] = jnp.broadcast_to(numbers[0] * direction, (LANES,))
            whole_numbers[2 * at + 1, :] = jnp.broadcast_to(numbers[1], (LANES,))
            weights[pl.ds(at * taps, taps), :] = jnp.broadcast_to(chosen[:taps], (taps, LANES))


def level_part(index, direction, whole_numbers, weights, given, base, out):
    views, planes, columns = given.shape
    taps = weights.shape[0] // (whole_numbers.shape[0] // 2)
    count = columns // LANES
    rows = [index * views + v for v in range(views)]
    begins = [whole_numbers[2 * at, 0] for at in rows]
    sources = [whole_numbers[2 * at + 1, 0] for at in rows]
    sums = []
    for v, at in enumerate(rows):
        factors = [
            jnp.broadcast_to(weights[pl.ds(at * taps + k, 1), :], (planes, LANES))
            for k in range(taps)
        ]
        if direction > 0:
            sums.append(shifted_sum(given[sources[v]], begins[v], factors))
        else:
            sums.append(shifted_sum(given[v], begins[v] - (taps - 1), factors[::-1]))
    for m in range(views):
        for j in range(count):
            at = pl.ds(LANES * j, LANES)
            if direction > 0:
                total = sums[m][j]
            else:
                total = sum(jnp.where(sources[v] == m, sums[v][j], 0.0) for v in range(views))
            out[m, :, at] = total if base is None else base[m, :, at] + total


def part_kernel(index, direction, first, whole_numbers, weights, given, *refs):
    out = refs[-1]
    base = refs[0].at[:, pl.ds(first, out.shape[1])] if len(refs) == 2 else None
    level_part(index, direction, whole_numbers, weights, given, base, out)


def own_kernel(index, whole_numbers, weights, given, out, kept):
    level_part(index, 1, whole_numbers, weights, given, None, out)
    kept[...] = given[...]


def two_kernel(first, second, direction, whole_numbers, weights, given, base, other, out, between):
    level_part(first, direction, whole_numbers, weights, given, base, between)
    level_part(second, direction, whole_numbers, weights, between, other, out)


def halves_kernel(state, facing, rest):
    planes, width = state.shape[1], facing.shape[1]
    odd = lax.axis_index("slab") % 2
    facing[...] = state[:, pl.ds(pl.multiple_of(odd * (planes - width), width), width), :]
    rest[...] = state[:, pl.ds(pl.multiple_of((1 - odd) * width, width), planes - width), :]


def mix_kernel(reach, measured, ray, token, pair, across):
    width = 2 * reach
    odd = lax.axis_index("slab") % 2
    row = lax.broadcasted_iota(jnp.int32, pair.shape, 1)
    for mixed, top in ((pair, 1 - odd), (across, odd)):
        edge = pl.ds(pl.multiple_of(top * (measured.shape[1] - width), width), width)
        own = (row >= reach) == (top == 1)
        mixed[...] = jnp.where(own, measured[:, edge], pltpu.roll(ray[:, edge], reach, 1))


def edge_kernel(reach, beyond, index, whole_numbers, weights, given, base, out, message):
    level_part(index, 1, whole_numbers, weights, given, base, out)
    width = 2 * reach
    odd = lax.axis_index("slab") % 2
    top = odd if beyond else 1 - odd
    last = pl.multiple_of(top * (out.shape[1] - width), width)
    message[...] = out[:, pl.ds(last, width), :]


def tilt_kernel(
    cone, rest, facing, pair, across, pair_mix, across_mix, measured, ray, residual, cotangent, wide, seen, lengths, weighted
):
    views, planes, columns = measured.shape
    width = facing.shape[1]
    reach = width // 2
    crossed = cone.shape[0] // views
    slab = lax.axis_index("slab")
    odd = slab % 2
    at_end = (slab == 0) | (slab == lax.axis_size("slab") - 1)
    far = planes + width
    extended = planes + 2 * reach
    own = pl.ds(width, planes)
    at_facing = pl.ds(pl.multiple_of(width + odd * (planes - width), width), width)
    at_rest = pl.ds(pl.multiple_of(width + (1 - odd) * width, width), planes - width)
    for v in range(views):
        factors = [cone[pl.ds(v * crossed + e, 1), :] for e in range(crossed)]
        for j in range(columns // LANES):
            at = pl.ds(LANES * j, LANES)
            wide[v, j, at_facing] = facing[v, :, at]
            wide[v, j, at_rest] = rest[v, :, at]
            seen[v, j, own] = measured[v, :, at]
            lengths[v, j, own] = ray[v, :, at]
            for message, mixture, side, outside in (
                (pair, pair_mix, 1 - odd, False),
                (across, across_mix, odd, at_end),
            ):
                edge = pl.ds(pl.multiple_of(side * far, width), width)
                mixed = jnp.where(outside, 0.0, mixture[v, :, at])
                wide[v, j, edge] = jnp.where(outside, 0.0, message[v, :, at])
                seen[v, j, edge] = mixed
                lengths[v, j, edge] = pltpu.roll(mixed, reach, 0)
            total = factors[0] * wide[v, j, pl.ds(0, extended)]
            for e in range(1, crossed):
                total = total + factors[e] * wide[v, j, pl.ds(e, extended)]
            left = seen[v, j, pl.ds(reach, extended)] - total
            weighted[v, j] = lengths[v, j, pl.ds(reach, extended)] * left
            residual[v, :, at] = left[reach : reach + planes]
            total = factors[0] * weighted[v, j, pl.ds(2 * reach, planes)]
            for e in range(1, crossed):
                total = total + factors[e] * weighted[v, j, pl.ds(2 * reach - e, planes)]
            cotangent[v, :, at] = total


def copy_kernel(given, out):
    out[...] = given[...]


def shaped(*shape, dtype=jnp.float32):
    return jax.ShapeDtypeStruct(shape, dtype)


def call(kernel, out_shape, *args, scratch=(), name):
    return pl.pallas_call(
        kernel,
        out_shape=out_shape,
        in_specs=[BLOCK] * len(args),
        out_specs=jax.tree.map(lambda _: BLOCK, out_shape),
        scratch_shapes=scratch,
        compiler_params=SMALL,
        name=name,
    )(*args)


def across_view(x, apart):
    return lax.ppermute(x, "view", [(i, i ^ apart) for i in range(lax.axis_size("view"))])


def with_pair(x):
    return lax.ppermute(x, "slab", [(i, i ^ 1) for i in range(lax.axis_size("slab"))])


def across_pairs(x):
    views, count = lax.axis_size("view"), lax.axis_size("slab")
    moves = []
    for v in range(views):
        for i in range(count):
            beyond = i + 1 if i % 2 else i - 1
            to = (v, beyond) if 0 <= beyond < count else (v ^ 1, i)
            moves.append((v * count + i, to[0] * count + to[1]))
    return lax.ppermute(x, ("view", "slab"), moves)


def body(leaf_coeffs, measured, ray_weight, cone_weight, interp_weight, shift_offset, source_view):
    views, planes, columns = leaf_coeffs.shape
    crossed = cone_weight.shape[1]
    reach = crossed // 2
    taps = interp_weight.shape[3]
    level_count = lax.axis_size("view").bit_length() - 1
    groups = [(i, i + 1) for i in range(0, level_count - 2, 2)]
    groups += [(i,) for i in range(2 * len(groups), level_count)]
    whole = shaped(views, planes, columns)
    message = shaped(views, 2 * reach, columns)
    assert 2 * reach == 8 and planes % 16 == 0 and columns % LANES == 0

    entries = []

    def entry(level, channel, apart, direction):
        entries.append((level, channel, apart, direction))
        return len(entries) - 1

    forward_entries, back_entries = {}, {}
    for levels in groups:
        low, high = levels[0], levels[-1]
        shapes = [(low, 0), (low, 1)]
        if len(levels) == 2:
            shapes = [(low, 0), (low, 1 << high), (high, 0)]
            backs = [(high, 0), (high, 1 << low), (low, 0)]
        else:
            shapes = backs = [(low, 0)]
        forward_entries[levels] = [
            [entry(level, channel, apart, 1) for channel in (0, 1)] for level, apart in shapes
        ]
        back_entries[levels] = [
            [entry(level, channel, apart ^ (channel << level), -1) for channel in (0, 1)]
            for level, apart in backs
        ]
    packed = jnp.concatenate(
        [jnp.swapaxes(interp_weight, 2, 3)]
        + [x[:, :, None].astype(jnp.float32) for x in (shift_offset, source_view)],
        axis=2,
    )
    tables = call(
        functools.partial(table_kernel, entries, views),
        [
            shaped(len(entries) * views * 2, LANES, dtype=jnp.int32),
            shaped(len(entries) * views * taps, LANES),
        ],
        packed,
        name="tables",
    )
    cone = jnp.broadcast_to(cone_weight.reshape(-1, 1), (views * crossed, LANES))

    def one(index, direction, given, base=None, first=0):
        return call(
            functools.partial(part_kernel, index, direction, first),
            shaped(*given.shape),
            *tables,
            given,
            *(() if base is None else (base,)),
            name="part",
        )

    def two(first, second, direction, given, base, other):
        return call(
            functools.partial(two_kernel, first, second, direction),
            shaped(*given.shape),
            *tables,
            given,
            base,
            other,
            scratch=[pltpu.VMEM(given.shape, jnp.float32)],
            name="two_parts",
        )

    kept = [leaf_coeffs]

    def begin(index, direction, state):
        if state is not leaf_coeffs:
            return one(index, direction, state)
        own, kept[0] = call(
            functools.partial(own_kernel, index), [whole, whole], *tables, state, name="own"
        )
        return own

    def forward_pair(steps, direction, state, first, second, third, base=None):
        own_steps, other_steps, joined = steps
        other = one(other_steps[1], direction, third)
        other = one(other_steps[0], direction, second, other)
        joined_sum = one(joined[1], direction, other, base)
        own = begin(own_steps[0], direction, state)
        return two(own_steps[1], joined[0], direction, first, own, joined_sum)

    def back_pair(steps, direction, state, first, second, third, base=None):
        own_steps, other_steps, joined = steps
        other = one(other_steps[1], direction, third)
        other = one(other_steps[0], direction, second, other)
        joined_sum = one(joined[1], direction, other, base)
        own = begin(own_steps[0], direction, state)
        return two(own_steps[1], joined[0], direction, first, own, joined_sum)

    state = leaf_coeffs
    for levels in groups[:-1]:
        steps = forward_entries[levels]
        near = 1 << levels[0]
        if len(levels) == 2:
            far = 1 << levels[1]
            received = [across_view(state, apart) for apart in (near, far, near + far)]
            state = forward_pair(steps, 1, state, *received)
        else:
            received = across_view(state, near)
            state = one(steps[0][1], 1, received, one(steps[0][0], 1, state))

    pair_mix, across_mix = call(
        functools.partial(mix_kernel, reach),
        [message, message],
        measured,
        ray_weight,
        kept[0],
        name="mix",
    )
    across_mix = across_pairs(across_mix)
    pair_mix = with_pair(pair_mix)

    own_step, partner_step = forward_entries[groups[-1]][0]
    width = 2 * reach
    halves = call(
        halves_kernel,
        [shaped(views, width, columns), shaped(views, planes - width, columns)],
        state,
        name="halves",
    )
    halves = halves[::-1]
    received = [across_view(half, 1 << groups[-1][0]) for half in halves]
    begun = [one(own_step, 1, half) for half in halves]
    (rest, to_pair), (facing, to_across) = [
        call(
            functools.partial(edge_kernel, reach, beyond, partner_step),
            [shaped(*half.shape), message],
            *tables,
            half,
            base,
            name="edge",
        )
        for beyond, half, base in zip((False, True), received, begun)
    ]
    from_pair = with_pair(to_pair)
    from_across = across_pairs(to_across)

    residual, cotangent = call(
        tilt_kernel,
        [whole, whole],
        cone,
        rest,
        facing,
        from_pair,
        from_across,
        pair_mix,
        across_mix,
        measured,
        ray_weight,
        scratch=[
            pltpu.VMEM((views, columns // LANES, planes + beyond * reach, LANES), jnp.float32)
            for beyond in (4, 4, 4, 2)
        ],
        name="tilt",
    )

    residual = call(copy_kernel, whole, residual, name="residual")

    state = cotangent
    for levels in reversed(groups):
        steps = back_entries[levels]
        near = 1 << levels[0]
        base = kept[0] if levels == groups[0] else None
        if len(levels) == 2:
            far = 1 << levels[1]
            received = [across_view(state, apart) for apart in (far, near, near + far)]
            state = back_pair(steps, -1, state, *received, base)
        else:
            received = across_view(state, near)
            state = one(steps[0][1], -1, received, one(steps[0][0], -1, state, base))
    return (residual, state)


def solution(mesh):
    in_specs = (
        P("view", "slab", None),
        P("view", "slab", None),
        P("view", "slab", None),
        P("view", None),
        P(),
        P(),
        P(),
    )
    out_specs = (P("view", "slab", None), P("view", "slab", None))
    return jax.shard_map(body, mesh=mesh, in_specs=in_specs, out_specs=out_specs, check_vma=False)
```

```python
import functools

import jax
import jax.numpy as jnp
from jax import lax
from jax.experimental import pallas as pl
from jax.experimental.pallas import tpu as pltpu
from jax.sharding import PartitionSpec as P

LANES = 128
BLOCK = pl.BlockSpec(memory_space=pltpu.VMEM)
SMALL = pltpu.CompilerParams(vmem_limit_bytes=8 << 20)


def shifted_sum(rows, move, weights):
    planes, columns = rows.shape
    count = columns // LANES
    tiles = [rows[:, LANES * j : LANES * (j + 1)] for j in range(count)]
    lane = lax.broadcasted_iota(jnp.int32, (planes, LANES), 1)
    nothing = jnp.zeros((planes, LANES), jnp.float32)
    total = [None] * count
    for k, weight in enumerate(weights):
        turned = [pltpu.roll(tile, (LANES - move - k) & (LANES - 1), 1) for tile in tiles]
        below = lane + (move + k) < 0
        above = lane + (move + k) >= LANES
        for j in range(count):
            left = turned[j - 1] if j > 0 else nothing
            right = turned[j + 1] if j + 1 < count else nothing
            term = weight * jnp.where(below, left, jnp.where(above, right, turned[j]))
            total[j] = term if total[j] is None else total[j] + term
    return total


def table_kernel(entries, views, packed, whole_numbers, weights):
    me = lax.axis_index("view")
    kinds, rows = packed.shape[2:]
    taps = kinds - 2
    lane = lax.broadcasted_iota(jnp.int32, (kinds, rows), 1)
    for index, (level, channel, apart, direction) in enumerate(entries):
        block = packed[level, channel]
        for v in range(views):
            at = index * views + v
            chosen = jnp.sum(
                jnp.where(lane == (me ^ apart) * views + v, block, 0.0), axis=1, keepdims=True
            )
            numbers = chosen[taps:].astype(jnp.int32)
            whole_numbers[2 * at, :] = jnp.broadcast_to(numbers[0] * direction, (LANES,))
            whole_numbers[2 * at + 1, :] = jnp.broadcast_to(numbers[1], (LANES,))
            weights[pl.ds(at * taps, taps), :] = jnp.broadcast_to(chosen[:taps], (taps, LANES))


def level_part(index, direction, whole_numbers, weights, given, base, out):
    views, planes, columns = given.shape
    taps = weights.shape[0] // (whole_numbers.shape[0] // 2)
    count = columns // LANES
    rows = [index * views + v for v in range(views)]
    begins = [whole_numbers[2 * at, 0] for at in rows]
    sources = [whole_numbers[2 * at + 1, 0] for at in rows]
    sums = []
    for v, at in enumerate(rows):
        factors = [
            jnp.broadcast_to(weights[pl.ds(at * taps + k, 1), :], (planes, LANES))
            for k in range(taps)
        ]
        if direction > 0:
            sums.append(shifted_sum(given[sources[v]], begins[v], factors))
        else:
            sums.append(shifted_sum(given[v], begins[v] - (taps - 1), factors[::-1]))
    for m in range(views):
        for j in range(count):
            at = pl.ds(LANES * j, LANES)
            if direction > 0:
                total = sums[m][j]
            else:
                total = sum(jnp.where(sources[v] == m, sums[v][j], 0.0) for v in range(views))
            out[m, :, at] = total if base is None else base[m, :, at] + total


def part_kernel(index, direction, first, whole_numbers, weights, given, *refs):
    out = refs[-1]
    base = refs[0].at[:, pl.ds(first, out.shape[1])] if len(refs) == 2 else None
    level_part(index, direction, whole_numbers, weights, given, base, out)


def own_kernel(index, whole_numbers, weights, given, out, kept):
    level_part(index, 1, whole_numbers, weights, given, None, out)
    kept[...] = given[...]


def two_kernel(first, second, direction, whole_numbers, weights, given, base, other, out, between):
    level_part(first, direction, whole_numbers, weights, given, base, between)
    level_part(second, direction, whole_numbers, weights, between, other, out)


def halves_kernel(state, facing, rest):
    planes, width = state.shape[1], facing.shape[1]
    odd = lax.axis_index("slab") % 2
    facing[...] = state[:, pl.ds(pl.multiple_of(odd * (planes - width), width), width), :]
    rest[...] = state[:, pl.ds(pl.multiple_of((1 - odd) * width, width), planes - width), :]


def mix_kernel(reach, measured, ray, token, pair, across):
    width = 2 * reach
    odd = lax.axis_index("slab") % 2
    row = lax.broadcasted_iota(jnp.int32, pair.shape, 1)
    for mixed, top in ((pair, 1 - odd), (across, odd)):
        edge = pl.ds(pl.multiple_of(top * (measured.shape[1] - width), width), width)
        own = (row >= reach) == (top == 1)
        mixed[...] = jnp.where(own, measured[:, edge], pltpu.roll(ray[:, edge], reach, 1))


def edge_kernel(reach, beyond, index, whole_numbers, weights, given, base, out, message):
    level_part(index, 1, whole_numbers, weights, given, base, out)
    width = 2 * reach
    odd = lax.axis_index("slab") % 2
    top = odd if beyond else 1 - odd
    last = pl.multiple_of(top * (out.shape[1] - width), width)
    message[...] = out[:, pl.ds(last, width), :]


def tilt_kernel(
    cone, rest, facing, pair, across, pair_mix, across_mix, measured, ray, residual, cotangent, wide, seen, lengths, weighted
):
    views, planes, columns = measured.shape
    width = facing.shape[1]
    reach = width // 2
    crossed = cone.shape[0] // views
    slab = lax.axis_index("slab")
    odd = slab % 2
    at_end = (slab == 0) | (slab == lax.axis_size("slab") - 1)
    far = planes + width
    extended = planes + 2 * reach
    own = pl.ds(width, planes)
    at_facing = pl.ds(pl.multiple_of(width + odd * (planes - width), width), width)
    at_rest = pl.ds(pl.multiple_of(width + (1 - odd) * width, width), planes - width)
    for v in range(views):
        factors = [cone[pl.ds(v * crossed + e, 1), :] for e in range(crossed)]
        for j in range(columns // LANES):
            at = pl.ds(LANES * j, LANES)
            wide[v, j, at_facing] = facing[v, :, at]
            wide[v, j, at_rest] = rest[v, :, at]
            seen[v, j, own] = measured[v, :, at]
            lengths[v, j, own] = ray[v, :, at]
            for message, mixture, side, outside in (
                (pair, pair_mix, 1 - odd, False),
                (across, across_mix, odd, at_end),
            ):
                edge = pl.ds(pl.multiple_of(side * far, width), width)
                mixed = jnp.where(outside, 0.0, mixture[v, :, at])
                wide[v, j, edge] = jnp.where(outside, 0.0, message[v, :, at])
                seen[v, j, edge] = mixed
                lengths[v, j, edge] = pltpu.roll(mixed, reach, 0)
            total = factors[0] * wide[v, j, pl.ds(0, extended)]
            for e in range(1, crossed):
                total = total + factors[e] * wide[v, j, pl.ds(e, extended)]
            left = seen[v, j, pl.ds(reach, extended)] - total
            weighted[v, j] = lengths[v, j, pl.ds(reach, extended)] * left
            residual[v, :, at] = left[reach : reach + planes]
            total = factors[0] * weighted[v, j, pl.ds(2 * reach, planes)]
            for e in range(1, crossed):
                total = total + factors[e] * weighted[v, j, pl.ds(2 * reach - e, planes)]
            cotangent[v, :, at] = total


def copy_kernel(given, out):
    out[...] = given[...]


def shaped(*shape, dtype=jnp.float32):
    return jax.ShapeDtypeStruct(shape, dtype)


def call(kernel, out_shape, *args, scratch=(), name):
    return pl.pallas_call(
        kernel,
        out_shape=out_shape,
        in_specs=[BLOCK] * len(args),
        out_specs=jax.tree.map(lambda _: BLOCK, out_shape),
        scratch_shapes=scratch,
        compiler_params=SMALL,
        cost_estimate=pl.CostEstimate(flops=10**8, bytes_accessed=2 * 10**6, transcendentals=0),
        name=name,
    )(*args)


def across_view(x, apart):
    return lax.ppermute(x, "view", [(i, i ^ apart) for i in range(lax.axis_size("view"))])


def with_pair(x):
    return lax.ppermute(x, "slab", [(i, i ^ 1) for i in range(lax.axis_size("slab"))])


def across_pairs(x):
    views, count = lax.axis_size("view"), lax.axis_size("slab")
    moves = []
    for v in range(views):
        for i in range(count):
            beyond = i + 1 if i % 2 else i - 1
            to = (v, beyond) if 0 <= beyond < count else (v ^ 1, i)
            moves.append((v * count + i, to[0] * count + to[1]))
    return lax.ppermute(x, ("view", "slab"), moves)


def body(leaf_coeffs, measured, ray_weight, cone_weight, interp_weight, shift_offset, source_view):
    views, planes, columns = leaf_coeffs.shape
    crossed = cone_weight.shape[1]
    reach = crossed // 2
    taps = interp_weight.shape[3]
    level_count = lax.axis_size("view").bit_length() - 1
    groups = [(i, i + 1) for i in range(0, level_count - 2, 2)]
    groups += [(i,) for i in range(2 * len(groups), level_count)]
    whole = shaped(views, planes, columns)
    message = shaped(views, 2 * reach, columns)
    assert 2 * reach == 8 and planes % 16 == 0 and columns % LANES == 0

    entries = []

    def entry(level, channel, apart, direction):
        entries.append((level, channel, apart, direction))
        return len(entries) - 1

    forward_entries, back_entries = {}, {}
    for levels in groups:
        low, high = levels[0], levels[-1]
        shapes = [(low, 0), (low, 1)]
        if len(levels) == 2:
            shapes = [(low, 0), (low, 1 << high), (high, 0)]
            backs = [(high, 0), (high, 1 << low), (low, 0)]
        else:
            shapes = backs = [(low, 0)]
        forward_entries[levels] = [
            [entry(level, channel, apart, 1) for channel in (0, 1)] for level, apart in shapes
        ]
        back_entries[levels] = [
            [entry(level, channel, apart ^ (channel << level), -1) for channel in (0, 1)]
            for level, apart in backs
        ]
    packed = jnp.concatenate(
        [jnp.swapaxes(interp_weight, 2, 3)]
        + [x[:, :, None].astype(jnp.float32) for x in (shift_offset, source_view)],
        axis=2,
    )
    tables = call(
        functools.partial(table_kernel, entries, views),
        [
            shaped(len(entries) * views * 2, LANES, dtype=jnp.int32),
            shaped(len(entries) * views * taps, LANES),
        ],
        packed,
        name="tables",
    )
    cone = jnp.broadcast_to(cone_weight.reshape(-1, 1), (views * crossed, LANES))

    def one(index, direction, given, base=None, first=0):
        return call(
            functools.partial(part_kernel, index, direction, first),
            shaped(*given.shape),
            *tables,
            given,
            *(() if base is None else (base,)),
            name="part",
        )

    def two(first, second, direction, given, base, other):
        return call(
            functools.partial(two_kernel, first, second, direction),
            shaped(*given.shape),
            *tables,
            given,
            base,
            other,
            scratch=[pltpu.VMEM(given.shape, jnp.float32)],
            name="two_parts",
        )

    kept = [leaf_coeffs]

    def begin(index, direction, state):
        if state is not leaf_coeffs:
            return one(index, direction, state)
        own, kept[0] = call(
            functools.partial(own_kernel, index), [whole, whole], *tables, state, name="own"
        )
        return own

    def forward_pair(steps, direction, state, first, second, third, base=None):
        own_steps, other_steps, joined = steps
        other = one(other_steps[1], direction, third)
        other = one(other_steps[0], direction, second, other)
        joined_sum = one(joined[1], direction, other, base)
        own = begin(own_steps[0], direction, state)
        return two(own_steps[1], joined[0], direction, first, own, joined_sum)

    def back_pair(steps, direction, state, first, second, third, base=None):
        own_steps, other_steps, joined = steps
        other = one(other_steps[1], direction, third)
        other = one(other_steps[0], direction, second, other)
        joined_sum = one(joined[1], direction, other, base)
        own = begin(own_steps[0], direction, state)
        return two(own_steps[1], joined[0], direction, first, own, joined_sum)

    state = leaf_coeffs
    for levels in groups[:-1]:
        steps = forward_entries[levels]
        near = 1 << levels[0]
        if len(levels) == 2:
            far = 1 << levels[1]
            received = [across_view(state, apart) for apart in (near, far, near + far)]
            state = forward_pair(steps, 1, state, *received)
        else:
            received = across_view(state, near)
            state = one(steps[0][1], 1, received, one(steps[0][0], 1, state))

    pair_mix, across_mix = call(
        functools.partial(mix_kernel, reach),
        [message, message],
        measured,
        ray_weight,
        kept[0],
        name="mix",
    )
    across_mix = across_pairs(across_mix)
    pair_mix = with_pair(pair_mix)

    own_step, partner_step = forward_entries[groups[-1]][0]
    width = 2 * reach
    halves = call(
        halves_kernel,
        [shaped(views, width, columns), shaped(views, planes - width, columns)],
        state,
        name="halves",
    )
    halves = halves[::-1]
    received = [across_view(half, 1 << groups[-1][0]) for half in halves]
    begun = [one(own_step, 1, half) for half in halves]
    (rest, to_pair), (facing, to_across) = [
        call(
            functools.partial(edge_kernel, reach, beyond, partner_step),
            [shaped(*half.shape), message],
            *tables,
            half,
            base,
            name="edge",
        )
        for beyond, half, base in zip((False, True), received, begun)
    ]
    from_pair = with_pair(to_pair)
    from_across = across_pairs(to_across)

    residual, cotangent = call(
        tilt_kernel,
        [whole, whole],
        cone,
        rest,
        facing,
        from_pair,
        from_across,
        pair_mix,
        across_mix,
        measured,
        ray_weight,
        scratch=[
            pltpu.VMEM((views, columns // LANES, planes + beyond * reach, LANES), jnp.float32)
            for beyond in (4, 4, 4, 2)
        ],
        name="tilt",
    )

    residual = call(copy_kernel, whole, residual, name="residual")

    state = cotangent
    for levels in reversed(groups):
        steps = back_entries[levels]
        near = 1 << levels[0]
        base = kept[0] if levels == groups[0] else None
        if len(levels) == 2:
            far = 1 << levels[1]
            received = [across_view(state, apart) for apart in (far, near, near + far)]
            state = back_pair(steps, -1, state, *received, base)
        else:
            received = across_view(state, near)
            state = one(steps[0][1], -1, received, one(steps[0][0], -1, state, base))
    return (residual, state)


def solution(mesh):
    in_specs = (
        P("view", "slab", None),
        P("view", "slab", None),
        P("view", "slab", None),
        P("view", None),
        P(),
        P(),
        P(),
    )
    out_specs = (P("view", "slab", None), P("view", "slab", None))
    return jax.shard_map(body, mesh=mesh, in_specs=in_specs, out_specs=out_specs, check_vma=False)
```
